256 devices in a mesh: dp: 4 (over y), vocab: 64 (over x, z, core).
Axes of the slice: x: 4, y: 4, z: 8, core: 2. Of those that a mesh axis runs over, the one named last changes fastest.
Arguments:
- window_hidden_states: bfloat16 [1024, 4608], P('dp'), may hold values from -40 to 40
- output_head_weight: bfloat16 [196608, 4608], P(('dp', 'vocab')), may hold values from -0.044194174 to 0.044194174
- adapter_first_factor: bfloat16 [64, 4608], replicated, may hold values from -0.09375 to 0.09375
- adapter_second_factor: bfloat16 [196608, 64], P(('dp', 'vocab')), may hold values from -0.1875 to 0.1875
- first_factor_direction: bfloat16 [64, 4608], replicated, may hold values from -0.09375 to 0.09375
- second_factor_direction: bfloat16 [196608, 64], P(('dp', 'vocab')), may hold values from -0.75 to 0.75
Outputs:
- grad_a: float32 [64, 4608], replicated
- grad_b: float32 [196608, 64], P(('dp', 'vocab'))
The draws below stay inside these ranges and needn't reach their ends.
All inputs are finite; a program needn't handle non-finite values.
Results may differ from the reference program's by a relative error of at most 0.007.
Values may be sent and summed in bfloat16 or wider, within the bound.
A program may use at most 128 MiB of HBM per device.

```python
from functools import partial
import jax
import jax.numpy as jnp
from jax import lax

MODEL_WIDTH = 4608
ADAPTER_RANK = 64
VOCAB_PER_SHARD = 768
TOKENS = 1024
VOCAB_ENTRIES = 196608


def weight_row(key, row_index):
    values = jax.random.normal(jax.random.fold_in(jax.random.fold_in(key, 11), row_index), (MODEL_WIDTH,), jnp.float32)
    return jnp.clip(values, -3.0, 3.0) * MODEL_WIDTH ** (-0.5)


def draw_output_head_weight(key, part):
    row_ids = jnp.arange(VOCAB_ENTRIES)
    return jax.vmap(partial(weight_row, key))(row_ids).astype(jnp.bfloat16)


def draw_window_hidden_states(key, part):
    key = jax.random.fold_in(key, 3)
    states = jnp.clip(jax.random.normal(jax.random.fold_in(key, 1), (TOKENS, MODEL_WIDTH), jnp.float32), -4.0, 4.0) * 2.5
    return states.astype(jnp.bfloat16)


def shard_levels(rng, shape, cuts, smallest, top_value):
    level, own = 1.0, jax.random.fold_in(rng, 6)
    for axis_at, shards_of in cuts:
        draws = jnp.exp(jax.random.uniform(jax.random.fold_in(own, axis_at), (shards_of,), jnp.float32, smallest / len(cuts), top_value / len(cuts)))
        level = level * jnp.repeat(draws, shape[axis_at] // shards_of).reshape([-1 if axis == axis_at else 1 for axis in range(len(shape))])
    return level


def bell_draw(key, dims, scale, most, pieces=(), held_as=jnp.bfloat16):
    drawn = scale * jax.random.normal(key, dims, jnp.float32)
    if pieces:
        drawn = drawn * shard_levels(key, dims, pieces, -0.22, 0.18)
    return jnp.clip(drawn, -most, most).astype(held_as)


def setup_inputs(seed: int = 0) -> dict:
    splits = jax.random.split(jax.random.key(seed), 7)
    return {
        "window_hidden_states": draw_window_hidden_states(jax.random.fold_in(splits[6], 71), 0),
        "output_head_weight": draw_output_head_weight(jax.random.fold_in(splits[6], 71), 0),
        "adapter_first_factor": bell_draw(splits[2], (ADAPTER_RANK, MODEL_WIDTH), MODEL_WIDTH ** -0.5, 0.09375),
        "adapter_second_factor": bell_draw(splits[3], (VOCAB_ENTRIES, ADAPTER_RANK), (16 * ADAPTER_RANK) ** -0.5, 0.1875, ((0, 256),)),
        "first_factor_direction": bell_draw(splits[4], (ADAPTER_RANK, MODEL_WIDTH), MODEL_WIDTH ** -0.5, 0.09375),
        "second_factor_direction": bell_draw(splits[5], (VOCAB_ENTRIES, ADAPTER_RANK), ADAPTER_RANK ** -0.5, 0.75, ((0, 256),)),
    }


def reference(window_hidden_states, output_head_weight, adapter_first_factor, adapter_second_factor, first_factor_direction, second_factor_direction):
    reduced_rank_projection = jnp.dot(window_hidden_states, adapter_first_factor.T, preferred_element_type=jnp.float32).astype(jnp.bfloat16)
    low_tangent = jnp.dot(window_hidden_states, first_factor_direction.T, preferred_element_type=jnp.float32).astype(jnp.bfloat16)
    block_count = VOCAB_ENTRIES // VOCAB_PER_SHARD
    weight_blocks = output_head_weight.reshape(block_count, VOCAB_PER_SHARD, MODEL_WIDTH)
    factor_block_list = adapter_second_factor.reshape(block_count, VOCAB_PER_SHARD, ADAPTER_RANK)
    tangent_blocks = second_factor_direction.reshape(block_count, VOCAB_PER_SHARD, ADAPTER_RANK)

    def block_logits(w_block, b_block, db_block):
        vocab_logits = jnp.dot(window_hidden_states, w_block.T, preferred_element_type=jnp.float32)
        vocab_logits = vocab_logits + jnp.dot(reduced_rank_projection, b_block.T, preferred_element_type=jnp.float32)
        tangent_logits = jnp.dot(low_tangent, b_block.T, preferred_element_type=jnp.float32)
        tangent_logits = tangent_logits + jnp.dot(reduced_rank_projection, db_block.T, preferred_element_type=jnp.float32)
        return vocab_logits, tangent_logits

    def first_pass(carry, blocks_in):
        row_top, row_total, row_weighted = carry
        vocab_logits, tangent_logits = block_logits(blocks_in[0], blocks_in[1], blocks_in[2])
        new_top = jnp.maximum(row_top, jnp.max(vocab_logits, axis=1))
        decay = jnp.exp(row_top - new_top)
        exp_terms = jnp.exp(vocab_logits - new_top[:, None])
        row_total = row_total * decay + jnp.sum(exp_terms, axis=1)
        row_weighted = row_weighted * decay + jnp.sum(exp_terms * tangent_logits, axis=1)
        return (new_top, row_total, row_weighted), None

    start_state = (jnp.full((TOKENS,), -jnp.inf, jnp.float32), jnp.zeros((TOKENS,), jnp.float32), jnp.zeros((TOKENS,), jnp.float32))
    (row_top, row_total, row_weighted), unused = lax.scan(first_pass, start_state, (weight_blocks, factor_block_list, tangent_blocks))
    row_mean = row_weighted / row_total

    def second_pass(accum, blocks_in):
        vocab_logits, tangent_logits = block_logits(blocks_in[0], blocks_in[1], blocks_in[2])
        probs = jnp.exp(vocab_logits - row_top[:, None]) / row_total[:, None]
        curvature_product = (probs * (tangent_logits - row_mean[:, None])).astype(jnp.bfloat16)
        grad_block = jnp.dot(curvature_product.T, reduced_rank_projection, preferred_element_type=jnp.float32)
        return accum + jnp.dot(curvature_product, blocks_in[1], preferred_element_type=jnp.float32), grad_block

    column_sum, grad_blocks = lax.scan(second_pass, jnp.zeros((TOKENS, ADAPTER_RANK), jnp.float32), (weight_blocks, factor_block_list, tangent_blocks))
    grad_b = grad_blocks.reshape(VOCAB_ENTRIES, ADAPTER_RANK)
    grad_a = jnp.dot(column_sum.astype(jnp.bfloat16).T, window_hidden_states, preferred_element_type=jnp.float32)
    return grad_a, grad_b
```

```python
import jax
import jax.numpy as jnp
from jax import lax
from jax.experimental import pallas as pl
from jax.experimental.pallas import tpu as pltpu
from jax.sharding import PartitionSpec as P

MESH = pl.DeviceIdType.MESH
F32 = jnp.float32
BF16 = jnp.bfloat16

WIDTH = 4608
RANK = 64
VOCAB = 768
TOKENS = 1024
CHUNK = 256
ROWS = VOCAB + 2 * RANK
NX, NY, NZ = 4, 4, 8
DEPTH = 1536
BLOCK = 64
COLS = 512


def place(x, y, z, c):
    return (y, x * 16 + z * 2 + c)


def remote(src, dst, send_sem, recv_sem, device):
    return pltpu.make_async_remote_copy(
        src_ref=src,
        dst_ref=dst,
        send_sem=send_sem,
        recv_sem=recv_sem,
        device_id=device,
        device_id_type=MESH,
    )


def merge(parts):
    top = parts[0][0]
    for part in parts[1:]:
        top = jnp.maximum(top, part[0])
    scales = [jnp.exp(part[0] - top) for part in parts]
    total = scales[0] * parts[0][1]
    weighted = total * parts[0][2]
    for scale, part in zip(scales[1:], parts[1:]):
        share = scale * part[1]
        total = total + share
        weighted = weighted + share * part[2]
    mean = weighted / total
    moved = None
    plain = None
    for scale, part in zip(scales, parts):
        shift = scale * (part[2] - mean)
        one = scale * part[3] + shift * part[4]
        two = scale * part[4]
        moved = one if moved is None else moved + one
        plain = two if plain is None else plain + two
    return top, total, mean, moved, plain


def stat_rows(top, total, mean):
    return jnp.concatenate([top, total, mean, jnp.zeros((5, top.shape[1]), F32)], axis=0)


def kernel(
    s_ref, w_ref, a_ref, ad_ref, bt_ref, dbt_ref, ga_ref, gb_ref,
    wall, sg, acc, e_buf, t_buf, xr, bl, bt2, h1, h2, hs, cfull,
    p0, r1, p1, r2, r3, cg, stg,
    load_sem, ys, yr, gs, gr, ss1, sr1, xs, xrv, zs, zr, cs, cr, ts, tr, fs, fr,
):
    y = lax.axis_index("dp")
    v = lax.axis_index("vocab")
    x, z, c = v // 16, (v // 2) % 8, v % 2
    sib = place(x, y, z, 1 - c)
    y_up, y_down = place(x, (y + 1) % NY, z, c), place(x, (y + 3) % NY, z, c)
    pairs = [(dx, dy) for dx in range(NX) for dy in range(NY) if (dx, dy) != (0, 0)]
    xy = [((x + dx) % NX, (y + dy) % NY) for dx, dy in pairs]

    barrier = pltpu.get_barrier_semaphore()
    everyone = [sib] + [place(px, py, z, c) for px, py in xy] + [place(x, y, (z + d) % NZ, c) for d in range(1, NZ)]
    for peer in everyone:
        pl.semaphore_signal(barrier, 1, device_id=peer, device_id_type=MESH)

    def rows_of(j, start, size):
        return sg.at[pl.ds(pl.multiple_of(j * CHUNK + start, 16), size)]

    loads = [
        pltpu.make_async_copy(s_ref, rows_of(y, 0, CHUNK), load_sem.at[0]),
        pltpu.make_async_copy(w_ref, wall.at[pl.ds(0, VOCAB)], load_sem.at[1]),
        pltpu.make_async_copy(a_ref, wall.at[pl.ds(VOCAB, RANK)], load_sem.at[2]),
        pltpu.make_async_copy(ad_ref, wall.at[pl.ds(VOCAB + RANK, RANK)], load_sem.at[3]),
    ]
    for load in loads:
        load.start()

    bt = bt_ref[...].astype(F32)
    dbt = dbt_ref[...].astype(F32)
    bl[...] = jnp.concatenate([bt, jnp.zeros_like(bt)], axis=0).T.astype(BF16)
    bt2[...] = jnp.concatenate([dbt, bt], axis=0).T.astype(BF16)

    pl.semaphore_wait(barrier, len(everyone))

    half = c * (CHUNK // 2)
    quarter = CHUNK // 4
    before, after, across = (y + 3) % NY, (y + 1) % NY, (y + 2) % NY
    mine = s_ref.at[pl.ds(pl.multiple_of(half, 16), CHUNK // 2)]
    sends = [
        remote(mine, rows_of(y, half, CHUNK // 2), ys.at[0], yr.at[0], y_up),
        remote(mine, rows_of(y, half, CHUNK // 2), ys.at[1], yr.at[1], y_down),
    ]
    for send in sends:
        send.start()

    def arrived(ref, send_sem, recv_sem):
        remote(ref, ref, send_sem, recv_sem, sib).wait_recv()

    def pass_on(j, k):
        held = rows_of(j, half, CHUNK // 2)
        copy = remote(held, held, gs.at[k], gr.at[k], sib)
        copy.start()
        sends.append(copy)

    def whole(j, k):
        arrived(rows_of(j, CHUNK // 2 - half, CHUNK // 2), gs.at[k], gr.at[k])

    def compute(j):
        first = pl.multiple_of(j * CHUNK, CHUNK)
        here = pl.ds(first, CHUNK)

        def deep(k, carry):
            at = pl.ds(pl.multiple_of(k * DEPTH, 128), DEPTH)
            part = lax.dot_general(wall[:, at], sg[here, at], (((1,), (1,)), ((), ())), preferred_element_type=F32)

            @pl.when(k == 0)
            def _():
                acc[...] = part

            @pl.when(k > 0)
            def _():
                acc[...] += part

            return carry

        lax.fori_loop(0, WIDTH // DEPTH, deep, 0)
        xr[:, here] = acc[VOCAB:ROWS, :].astype(BF16)

        def logits(i, top):
            at = pl.ds(pl.multiple_of(i * BLOCK, BLOCK), BLOCK)
            low = xr[:, here]
            row = acc[at, :] + jnp.dot(bl[at, :], low, preferred_element_type=F32)
            e_buf[at, here] = row
            t_buf[at, here] = jnp.dot(bt2[at, :], low, preferred_element_type=F32)
            return jnp.maximum(top, jnp.max(row.reshape(BLOCK // 8, 8, CHUNK), axis=0))

        top = lax.fori_loop(0, VOCAB // BLOCK, logits, jnp.full((8, CHUNK), -jnp.inf, F32))
        top = jnp.max(top, axis=0, keepdims=True)

        def sums(i, carry):
            at = pl.ds(pl.multiple_of(i * BLOCK, BLOCK), BLOCK)
            e = jnp.exp(e_buf[at, here] - top)
            e_buf[at, here] = e
            et = e * t_buf[at, here]
            return (
                carry[0] + jnp.sum(e.reshape(BLOCK // 8, 8, CHUNK), axis=0),
                carry[1] + jnp.sum(et.reshape(BLOCK // 8, 8, CHUNK), axis=0),
            )

        zero = jnp.zeros((8, CHUNK), F32)
        total, weighted = lax.fori_loop(0, VOCAB // BLOCK, sums, (zero, zero))
        total = jnp.sum(total, axis=0, keepdims=True)
        mean = jnp.sum(weighted, axis=0, keepdims=True) / total

        def rounded(i, carry):
            at = pl.ds(pl.multiple_of(i * BLOCK, BLOCK), BLOCK)
            e = e_buf[at, here]
            h1[at, :] = (e * (t_buf[at, here] - mean)).astype(BF16)
            h2[at, :] = e.astype(BF16)
            return carry

        lax.fori_loop(0, VOCAB // BLOCK, rounded, 0)
        side, there = j // 2, pl.ds(pl.multiple_of((j % 2) * CHUNK, CHUNK), CHUNK)
        p0[side, 0:RANK, there] = jnp.dot(bt_ref[...], h1[...], preferred_element_type=F32)
        p0[side, RANK : 2 * RANK, there] = jnp.dot(bt_ref[...], h2[...], preferred_element_type=F32)
        p0[side, 2 * RANK : 2 * RANK + 8, there] = stat_rows(top, total, mean)

    for load in loads:
        load.wait()
    compute(y)
    arrived(rows_of(before, half, CHUNK // 2), ys.at[0], yr.at[0])
    held = rows_of(before, half, quarter)
    sends.append(remote(held, held, ys.at[2], yr.at[2], y_up))
    sends[-1].start()
    pass_on(before, 0)
    arrived(rows_of(after, half, CHUNK // 2), ys.at[1], yr.at[1])
    held = rows_of(after, half + quarter, quarter)
    sends.append(remote(held, held, ys.at[3], yr.at[3], y_down))
    sends[-1].start()
    pass_on(after, 1)
    whole(before, 0)
    compute(before)
    whole(after, 1)
    compute(after)
    arrived(rows_of(across, half, quarter), ys.at[2], yr.at[2])
    arrived(rows_of(across, half + quarter, quarter), ys.at[3], yr.at[3])
    pass_on(across, 2)
    whole(across, 2)
    compute(across)

    copy = remote(p0.at[1 - c], r1, ss1.at[0], sr1.at[0], sib)
    copy.start()
    sends.append(copy)
    copy.wait_recv()
    for tx in range(NX):
        lanes = pl.ds(tx * 128, 128)

        def stats(ref, row):
            return ref[pl.ds(row, 1), lanes]

        own, other = p0.at[c], r1
        for ty in range(NY):
            g1, g2 = pl.ds(ty * 16, 16), pl.ds(RANK + ty * 16, 16)
            out = merge(
                [
                    (stats(ref, 128), stats(ref, 129), stats(ref, 130), ref[g1, lanes], ref[g2, lanes])
                    for ref in (own, other)
                ]
            )
            p1[tx * NY + ty] = jnp.concatenate([out[3], out[4], stat_rows(*out[:3])], axis=0)

    def unpack(ref, k):
        return (ref[k, 32:33], ref[k, 33:34], ref[k, 34:35], ref[k, 0:16], ref[k, 16:32])

    me = x * NY + y
    copies = []
    for k, (px, py) in enumerate(xy):
        copies.append(remote(p1.at[px * NY + py], r2.at[me], xs.at[k], xrv.at[k], place(px, py, z, c)))
        copies[-1].start()
    sends += copies
    r2[me] = p1[me]
    for k, (dx, dy) in enumerate(pairs):
        origin = ((x - dx + NX) % NX) * NY + (y - dy + NY) % NY
        arrived(r2.at[origin], xs.at[k], xrv.at[k])
    out = merge([unpack(r2, k) for k in range(NX * NY)])
    r3[z] = jnp.concatenate([out[3], out[4], stat_rows(*out[:3])], axis=0)
    for d in range(1, NZ):
        copy = remote(r3.at[z], r3.at[z], zs.at[d - 1], zr.at[d - 1], place(x, y, (z + d) % NZ, c))
        copy.start()
        sends.append(copy)
    for d in range(1, NZ):
        arrived(r3.at[(z - d + NZ) % NZ], zs.at[d - 1], zr.at[d - 1])
    top, total, mean, moved, plain = merge([unpack(r3, k) for k in range(NZ)])

    slot = c * NX + x
    strip = cg.at[slot, pl.ds(pl.multiple_of(y * 16, 16), 16)]
    strip[...] = (moved / total).astype(BF16)
    stg[slot] = stat_rows(top, total, mean)
    for d in range(1, NX):
        copy = remote(stg.at[slot], stg.at[slot], ts.at[d - 1], tr.at[d - 1], place((x + d) % NX, y, z, c))
        copy.start()
        sends.append(copy)
    for k, (px, py) in enumerate(xy):
        copy = remote(strip, strip, cs.at[k], cr.at[k], place(px, py, z, c))
        copy.start()
        sends.append(copy)
    for d in range(1, NX):
        arrived(stg.at[c * NX + (x - d + NX) % NX], ts.at[d - 1], tr.at[d - 1])
    held = stg.at[pl.ds(c * NX, NX)]
    copy = remote(held, held, fs.at[0], fr.at[0], sib)
    copy.start()
    sends.append(copy)
    for k, (dx, dy) in enumerate(pairs):
        from_x, from_y = (x - dx + NX) % NX, (y - dy + NY) % NY
        arrived(cg.at[c * NX + from_x, pl.ds(pl.multiple_of(from_y * 16, 16), 16)], cs.at[k], cr.at[k])
    held = cg.at[pl.ds(c * NX, NX)]
    copy = remote(held, held, fs.at[1], fr.at[1], sib)
    copy.start()
    sends.append(copy)
    arrived(stg.at[pl.ds((1 - c) * NX, NX)], fs.at[0], fr.at[0])

    factors, means = [], []
    for t in range(8):
        local_top = p0[t // 4, 128:129, (t % 4) * 128 : (t % 4 + 1) * 128]
        factors.append(jnp.exp(local_top - stg[t, 0:1]) / stg[t, 1:2])
        means.append(stg[t, 2:3])

    def hessian(i, carry):
        at = pl.ds(pl.multiple_of(i * BLOCK, BLOCK), BLOCK)
        for t in range(8):
            lanes = pl.ds(t * 128, 128)
            probs = e_buf[at, lanes] * factors[t]
            hs[at, lanes] = (probs * (t_buf[at, lanes] - means[t])).astype(BF16)
        return carry

    lax.fori_loop(0, VOCAB // BLOCK, hessian, 0)
    gb_ref[...] = lax.dot_general(xr[0:RANK, :], hs[...], (((1,), (1,)), ((), ())), preferred_element_type=F32)

    arrived(cg.at[pl.ds((1 - c) * NX, NX)], fs.at[1], fr.at[1])
    for t in range(8):
        cfull[:, t * 128 : (t + 1) * 128] = cg[t]

    def outer(n, carry):
        at = pl.ds(pl.multiple_of(n * COLS, 128), COLS)
        ga_ref[:, at] = jnp.dot(cfull[...], sg[:, at], preferred_element_type=F32)
        return carry

    lax.fori_loop(0, WIDTH // COLS, outer, 0)
    for send in sends:
        send.wait_send()


def shards(states, weight, first, second, first_direction, second_direction):
    vmem = pl.BlockSpec(memory_space=pltpu.VMEM)
    hbm = pl.BlockSpec(memory_space=pl.ANY)
    dma = pltpu.SemaphoreType.DMA
    grad_a, grad_b = pl.pallas_call(
        kernel,
        out_shape=(jax.ShapeDtypeStruct((RANK, WIDTH), F32), jax.ShapeDtypeStruct((RANK, VOCAB), F32)),
        in_specs=[hbm, hbm, hbm, hbm, vmem, vmem],
        out_specs=(vmem, vmem),
        scratch_shapes=[
            pltpu.VMEM((ROWS, WIDTH), BF16),
            pltpu.VMEM((TOKENS, WIDTH), BF16),
            pltpu.VMEM((ROWS, CHUNK), F32),
            pltpu.VMEM((VOCAB, TOKENS), F32),
            pltpu.VMEM((VOCAB, TOKENS), F32),
            pltpu.VMEM((2 * RANK, TOKENS), BF16),
            pltpu.VMEM((VOCAB, 2 * RANK), BF16),
            pltpu.VMEM((VOCAB, 2 * RANK), BF16),
            pltpu.VMEM((VOCAB, CHUNK), BF16),
            pltpu.VMEM((VOCAB, CHUNK), BF16),
            pltpu.VMEM((VOCAB, TOKENS), BF16),
            pltpu.VMEM((RANK, TOKENS), BF16),
            pltpu.VMEM((2, 2 * RANK + 8, TOKENS // 2), F32),
            pltpu.VMEM((2 * RANK + 8, TOKENS // 2), F32),
            pltpu.VMEM((NX * NY, 40, 128), F32),
            pltpu.VMEM((NX * NY, 40, 128), F32),
            pltpu.VMEM((NZ, 40, 128), F32),
            pltpu.VMEM((2 * NX, RANK, 128), BF16),
            pltpu.VMEM((2 * NX, 8, 128), F32),
            dma((4,)),
            dma((4,)), dma((4,)),
            dma((3,)), dma((3,)),
            dma((1,)), dma((1,)),
            dma((15,)), dma((15,)),
            dma((7,)), dma((7,)),
            dma((15,)), dma((15,)),
            dma((3,)), dma((3,)),
            dma((2,)), dma((2,)),
        ],
        compiler_params=pltpu.CompilerParams(
            collective_id=0, has_side_effects=True, vmem_limit_bytes=56 * 1024 * 1024
        ),
        cost_estimate=pl.CostEstimate(flops=10_000_000_000, bytes_accessed=20_000_000, transcendentals=800_000),
    )(states, weight, first, first_direction, second.T, second_direction.T)
    return grad_a, grad_b.T


def solution(mesh):
    in_specs = (
        P("dp", None),
        P(("dp", "vocab"), None),
        P(),
        P(("dp", "vocab"), None),
        P(),
        P(("dp", "vocab"), None),
    )
    out_specs = (P(), P(("dp", "vocab"), None))
    return jax.shard_map(shards, mesh=mesh, in_specs=in_specs, out_specs=out_specs, check_vma=False)
```

```python
import jax
import jax.numpy as jnp
from jax import lax
from jax.experimental import pallas as pl
from jax.experimental.pallas import tpu as pltpu
from jax.sharding import PartitionSpec as P

MESH = pl.DeviceIdType.MESH
F32 = jnp.float32
BF16 = jnp.bfloat16

WIDTH = 4608
RANK = 64
VOCAB = 768
TOKENS = 1024
CHUNK = 256
ROWS = VOCAB + 2 * RANK
NX, NY, NZ = 4, 4, 8
HALF = 2304
PART = 64
BLOCK = 64
COLS = 512


def place(x, y, z, c):
    return (y, x * 16 + z * 2 + c)


def remote(src, dst, send_sem, recv_sem, device):
    return pltpu.make_async_remote_copy(
        src_ref=src,
        dst_ref=dst,
        send_sem=send_sem,
        recv_sem=recv_sem,
        device_id=device,
        device_id_type=MESH,
    )


def merge(parts):
    top = parts[0][0]
    for part in parts[1:]:
        top = jnp.maximum(top, part[0])
    scales = [jnp.exp(part[0] - top) for part in parts]
    total = scales[0] * parts[0][1]
    weighted = total * parts[0][2]
    for scale, part in zip(scales[1:], parts[1:]):
        share = scale * part[1]
        total = total + share
        weighted = weighted + share * part[2]
    mean = weighted / total
    moved = None
    plain = None
    for scale, part in zip(scales, parts):
        shift = scale * (part[2] - mean)
        one = scale * part[3] + shift * part[4]
        two = scale * part[4]
        moved = one if moved is None else moved + one
        plain = two if plain is None else plain + two
    return top, total, mean, moved, plain


def stat_rows(top, total, mean):
    return jnp.concatenate([top, total, mean, jnp.zeros((5, top.shape[1]), F32)], axis=0)


def kernel(
    s_ref, w_ref, a_ref, ad_ref, bt_ref, dbt_ref, ga_ref, gb_ref,
    wall, sg, acc, e_buf, t_buf, xr, bl, bt2, h1, h2, hs, cfull,
    p0, r1, p1, r2, r3, cg, stg,
    load_sem, ys, yr, ns, nr, gs, gr, ss1, sr1, xs, xrv, zs, zr, cs, cr, ts, tr, fs, fr,
):
    y = lax.axis_index("dp")
    v = lax.axis_index("vocab")
    x, z, c = v // 16, (v // 2) % 8, v % 2
    sib = place(x, y, z, 1 - c)
    y_up, y_down = place(x, (y + 1) % NY, z, c), place(x, (y + 3) % NY, z, c)
    pairs = [(dx, dy) for dx in range(NX) for dy in range(NY) if (dx, dy) != (0, 0)]
    xy = [((x + dx) % NX, (y + dy) % NY) for dx, dy in pairs]

    barrier = pltpu.get_barrier_semaphore()
    everyone = [sib] + [place(px, py, z, c) for px, py in xy] + [place(x, y, (z + d) % NZ, c) for d in range(1, NZ)]
    for peer in everyone:
        pl.semaphore_signal(barrier, 1, device_id=peer, device_id_type=MESH)

    def rows_of(j, start, size):
        return sg.at[pl.ds(pl.multiple_of(j * CHUNK + start, 16), size)]

    loads = [
        pltpu.make_async_copy(s_ref, rows_of(y, 0, CHUNK), load_sem.at[0]),
        pltpu.make_async_copy(w_ref, wall.at[pl.ds(0, VOCAB)], load_sem.at[1]),
        pltpu.make_async_copy(a_ref, wall.at[pl.ds(VOCAB, RANK)], load_sem.at[2]),
        pltpu.make_async_copy(ad_ref, wall.at[pl.ds(VOCAB + RANK, RANK)], load_sem.at[3]),
    ]
    for load in loads:
        load.start()

    bt = bt_ref[...].astype(F32)
    dbt = dbt_ref[...].astype(F32)
    bl[...] = jnp.concatenate([bt, jnp.zeros_like(bt)], axis=0).T.astype(BF16)
    bt2[...] = jnp.concatenate([dbt, bt], axis=0).T.astype(BF16)

    pl.semaphore_wait(barrier, len(everyone))

    colour = (x + z) % 2
    before, after, across = (y + 3) % NY, (y + 1) % NY, (y + 2) % NY
    steps = [(before, 0), (after, 1), (before, 1), (after, 0), (across, 0), (across, 1)]
    around = [
        place((x + 1) % NX, y, z, c),
        place((x + 3) % NX, y, z, c),
        place(x, y, (z + 1) % NZ, c),
        place(x, y, (z + 7) % NZ, c),
    ]
    sends = []

    def send(*args):
        copy = remote(*args)
        copy.start()
        sends.append(copy)

    def arrived(ref, send_sem, recv_sem):
        remote(ref, ref, send_sem, recv_sem, sib).wait_recv()

    def piece(j, core, shade, h, first=0, size=PART):
        row = pl.multiple_of(j * CHUNK + (core * 2 + shade) * PART + first, 16)
        return sg.at[pl.ds(row, size), pl.ds(h * HALF, HALF)]

    def start_y(k, h, device):
        row = pl.multiple_of((c * 2 + colour) * PART, 16)
        send(s_ref.at[pl.ds(row, PART), pl.ds(h * HALF, HALF)], piece(y, c, colour, h), ys.at[k], yr.at[k], device)

    def from_y(k):
        j, h = steps[k]
        held = piece(j, c, colour, h)
        arrived(held, ys.at[k], yr.at[k])
        if k == 0:
            send(held, held, ys.at[4], yr.at[4], y_up)
        if k == 1:
            send(held, held, ys.at[5], yr.at[5], y_down)
        for i, device in enumerate(around):
            part = piece(j, c, colour, h, 16 * i, 16)
            send(part, part, ns.at[k * 4 + i], nr.at[k * 4 + i], device)
        send(held, held, gs.at[k * 2], gr.at[k * 2], sib)

    def from_around(k):
        j, h = steps[k]
        for i in range(4):
            arrived(piece(j, c, 1 - colour, h, 16 * i, 16), ns.at[k * 4 + i], nr.at[k * 4 + i])
        held = piece(j, c, 1 - colour, h)
        send(held, held, gs.at[k * 2 + 1], gr.at[k * 2 + 1], sib)

    def from_sib(k):
        j, h = steps[k]
        arrived(piece(j, 1 - c, colour, h), gs.at[k * 2], gr.at[k * 2])
        arrived(piece(j, 1 - c, 1 - colour, h), gs.at[k * 2 + 1], gr.at[k * 2 + 1])

    start_y(0, 0, y_up)
    start_y(1, 1, y_down)
    start_y(2, 1, y_up)
    start_y(3, 0, y_down)

    def product(j, h):
        here, at = pl.ds(pl.multiple_of(j * CHUNK, CHUNK), CHUNK), pl.ds(h * HALF, HALF)
        return lax.dot_general(wall[:, at], sg[here, at], (((1,), (1,)), ((), ())), preferred_element_type=F32)

    def finish(j, acc):
        first = pl.multiple_of(j * CHUNK, CHUNK)
        here = pl.ds(first, CHUNK)

        xr[:, here] = acc[VOCAB:ROWS, :].astype(BF16)

        def logits(i, top):
            at = pl.ds(pl.multiple_of(i * BLOCK, BLOCK), BLOCK)
            low = xr[:, here]
            row = acc[at, :] + jnp.dot(bl[at, :], low, preferred_element_type=F32)
            e_buf[at, here] = row
            t_buf[at, here] = jnp.dot(bt2[at, :], low, preferred_element_type=F32)
            return jnp.maximum(top, jnp.max(row.reshape(BLOCK // 8, 8, CHUNK), axis=0))

        top = lax.fori_loop(0, VOCAB // BLOCK, logits, jnp.full((8, CHUNK), -jnp.inf, F32))
        top = jnp.max(top, axis=0, keepdims=True)

        def sums(i, carry):
            at = pl.ds(pl.multiple_of(i * BLOCK, BLOCK), BLOCK)
            e = jnp.exp(e_buf[at, here] - top)
            e_buf[at, here] = e
            et = e * t_buf[at, here]
            return (
                carry[0] + jnp.sum(e.reshape(BLOCK // 8, 8, CHUNK), axis=0),
                carry[1] + jnp.sum(et.reshape(BLOCK // 8, 8, CHUNK), axis=0),
            )

        zero = jnp.zeros((8, CHUNK), F32)
        total, weighted = lax.fori_loop(0, VOCAB // BLOCK, sums, (zero, zero))
        total = jnp.sum(total, axis=0, keepdims=True)
        mean = jnp.sum(weighted, axis=0, keepdims=True) / total

        def rounded(i, carry):
            at = pl.ds(pl.multiple_of(i * BLOCK, BLOCK), BLOCK)
            e = e_buf[at, here]
            h1[at, :] = (e * (t_buf[at, here] - mean)).astype(BF16)
            h2[at, :] = e.astype(BF16)
            return carry

        lax.fori_loop(0, VOCAB // BLOCK, rounded, 0)
        side, there = j // 2, pl.ds(pl.multiple_of((j % 2) * CHUNK, CHUNK), CHUNK)
        p0[side, 0:RANK, there] = jnp.dot(bt_ref[...], h1[...], preferred_element_type=F32)
        p0[side, RANK : 2 * RANK, there] = jnp.dot(bt_ref[...], h2[...], preferred_element_type=F32)
        p0[side, 2 * RANK : 2 * RANK + 8, there] = stat_rows(top, total, mean)

    for load in loads:
        load.wait()
    first_acc, second_acc = acc.at[0], acc.at[1]
    here = pl.ds(pl.multiple_of(y * CHUNK, CHUNK), CHUNK)
    first_acc[...] = lax.dot_general(wall[...], sg[here, :], (((1,), (1,)), ((), ())), preferred_element_type=F32)
    finish(y, first_acc)
    from_y(0)
    from_y(1)
    from_around(0)
    from_around(1)
    from_y(2)
    from_y(3)
    from_sib(0)
    first_acc[...] = product(before, 0)
    from_sib(1)
    second_acc[...] = product(after, 1)
    from_around(2)
    from_around(3)
    from_y(4)
    from_y(5)
    from_sib(2)
    first_acc[...] += product(before, 1)
    from_sib(3)
    second_acc[...] += product(after, 0)
    finish(before, first_acc)
    from_around(4)
    from_around(5)
    finish(after, second_acc)
    from_sib(4)
    first_acc[...] = product(across, 0)
    from_sib(5)
    first_acc[...] += product(across, 1)
    finish(across, first_acc)

    copy = remote(p0.at[1 - c], r1, ss1.at[0], sr1.at[0], sib)
    copy.start()
    sends.append(copy)
    copy.wait_recv()
    for tx in range(NX):
        lanes = pl.ds(tx * 128, 128)

        def stats(ref, row):
            return ref[pl.ds(row, 1), lanes]

        own, other = p0.at[c], r1
        for ty in range(NY):
            g1, g2 = pl.ds(ty * 16, 16), pl.ds(RANK + ty * 16, 16)
            out = merge(
                [
                    (stats(ref, 128), stats(ref, 129), stats(ref, 130), ref[g1, lanes], ref[g2, lanes])
                    for ref in (own, other)
                ]
            )
            p1[tx * NY + ty] = jnp.concatenate([out[3], out[4], stat_rows(*out[:3])], axis=0)

    def unpack(ref, k):
        return (ref[k, 32:33], ref[k, 33:34], ref[k, 34:35], ref[k, 0:16], ref[k, 16:32])

    me = x * NY + y
    copies = []
    for k, (px, py) in enumerate(xy):
        copies.append(remote(p1.at[px * NY + py], r2.at[me], xs.at[k], xrv.at[k], place(px, py, z, c)))
        copies[-1].start()
    sends += copies
    r2[me] = p1[me]
    for k, (dx, dy) in enumerate(pairs):
        origin = ((x - dx + NX) % NX) * NY + (y - dy + NY) % NY
        arrived(r2.at[origin], xs.at[k], xrv.at[k])
    out = merge([unpack(r2, k) for k in range(NX * NY)])
    r3[z] = jnp.concatenate([out[3], out[4], stat_rows(*out[:3])], axis=0)
    for d in range(1, NZ):
        copy = remote(r3.at[z], r3.at[z], zs.at[d - 1], zr.at[d - 1], place(x, y, (z + d) % NZ, c))
        copy.start()
        sends.append(copy)
    for d in range(1, NZ):
        arrived(r3.at[(z - d + NZ) % NZ], zs.at[d - 1], zr.at[d - 1])
    top, total, mean, moved, plain = merge([unpack(r3, k) for k in range(NZ)])

    slot = c * NX + x
    strip = cg.at[slot, pl.ds(pl.multiple_of(y * 16, 16), 16)]
    strip[...] = (moved / total).astype(BF16)
    stg[slot] = stat_rows(top, total, mean)
    for d in range(1, NX):
        copy = remote(stg.at[slot], stg.at[slot], ts.at[d - 1], tr.at[d - 1], place((x + d) % NX, y, z, c))
        copy.start()
        sends.append(copy)
    for k, (px, py) in enumerate(xy):
        copy = remote(strip, strip, cs.at[k], cr.at[k], place(px, py, z, c))
        copy.start()
        sends.append(copy)
    for d in range(1, NX):
        arrived(stg.at[c * NX + (x - d + NX) % NX], ts.at[d - 1], tr.at[d - 1])
    held = stg.at[pl.ds(c * NX, NX)]
    copy = remote(held, held, fs.at[0], fr.at[0], sib)
    copy.start()
    sends.append(copy)
    for k, (dx, dy) in enumerate(pairs):
        from_x, from_y = (x - dx + NX) % NX, (y - dy + NY) % NY
        arrived(cg.at[c * NX + from_x, pl.ds(pl.multiple_of(from_y * 16, 16), 16)], cs.at[k], cr.at[k])
    held = cg.at[pl.ds(c * NX, NX)]
    copy = remote(held, held, fs.at[1], fr.at[1], sib)
    copy.start()
    sends.append(copy)
    arrived(stg.at[pl.ds((1 - c) * NX, NX)], fs.at[0], fr.at[0])

    factors, means = [], []
    for t in range(8):
        local_top = p0[t // 4, 128:129, (t % 4) * 128 : (t % 4 + 1) * 128]
        factors.append(jnp.exp(local_top - stg[t, 0:1]) / stg[t, 1:2])
        means.append(stg[t, 2:3])

    def hessian(i, carry):
        at = pl.ds(pl.multiple_of(i * BLOCK, BLOCK), BLOCK)
        for t in range(8):
            lanes = pl.ds(t * 128, 128)
            probs = e_buf[at, lanes] * factors[t]
            hs[at, lanes] = (probs * (t_buf[at, lanes] - means[t])).astype(BF16)
        return carry

    lax.fori_loop(0, VOCAB // BLOCK, hessian, 0)
    gb_ref[...] = lax.dot_general(xr[0:RANK, :], hs[...], (((1,), (1,)), ((), ())), preferred_element_type=F32)

    arrived(cg.at[pl.ds((1 - c) * NX, NX)], fs.at[1], fr.at[1])
    for t in range(8):
        cfull[:, t * 128 : (t + 1) * 128] = cg[t]

    def outer(n, carry):
        at = pl.ds(pl.multiple_of(n * COLS, 128), COLS)
        ga_ref[:, at] = jnp.dot(cfull[...], sg[:, at], preferred_element_type=F32)
        return carry

    lax.fori_loop(0, WIDTH // COLS, outer, 0)
    for copy in sends:
        copy.wait_send()


def shards(states, weight, first, second, first_direction, second_direction):
    vmem = pl.BlockSpec(memory_space=pltpu.VMEM)
    hbm = pl.BlockSpec(memory_space=pl.ANY)
    dma = pltpu.SemaphoreType.DMA
    grad_a, grad_b = pl.pallas_call(
        kernel,
        out_shape=(jax.ShapeDtypeStruct((RANK, WIDTH), F32), jax.ShapeDtypeStruct((RANK, VOCAB), F32)),
        in_specs=[hbm, hbm, hbm, hbm, vmem, vmem],
        out_specs=(vmem, vmem),
        scratch_shapes=[
            pltpu.VMEM((ROWS, WIDTH), BF16),
            pltpu.VMEM((TOKENS, WIDTH), BF16),
            pltpu.VMEM((2, ROWS, CHUNK), F32),
            pltpu.VMEM((VOCAB, TOKENS), F32),
            pltpu.VMEM((VOCAB, TOKENS), F32),
            pltpu.VMEM((2 * RANK, TOKENS), BF16),
            pltpu.VMEM((VOCAB, 2 * RANK), BF16),
            pltpu.VMEM((VOCAB, 2 * RANK), BF16),
            pltpu.VMEM((VOCAB, CHUNK), BF16),
            pltpu.VMEM((VOCAB, CHUNK), BF16),
            pltpu.VMEM((VOCAB, TOKENS), BF16),
            pltpu.VMEM((RANK, TOKENS), BF16),
            pltpu.VMEM((2, 2 * RANK + 8, TOKENS // 2), F32),
            pltpu.VMEM((2 * RANK + 8, TOKENS // 2), F32),
            pltpu.VMEM((NX * NY, 40, 128), F32),
            pltpu.VMEM((NX * NY, 40, 128), F32),
            pltpu.VMEM((NZ, 40, 128), F32),
            pltpu.VMEM((2 * NX, RANK, 128), BF16),
            pltpu.VMEM((2 * NX, 8, 128), F32),
            dma((4,)),
            dma((6,)), dma((6,)),
            dma((24,)), dma((24,)),
            dma((12,)), dma((12,)),
            dma((1,)), dma((1,)),
            dma((15,)), dma((15,)),
            dma((7,)), dma((7,)),
            dma((15,)), dma((15,)),
            dma((3,)), dma((3,)),
            dma((2,)), dma((2,)),
        ],
        compiler_params=pltpu.CompilerParams(
            collective_id=0, has_side_effects=True, vmem_limit_bytes=56 * 1024 * 1024
        ),
        cost_estimate=pl.CostEstimate(flops=10_000_000_000, bytes_accessed=20_000_000, transcendentals=800_000),
    )(states, weight, first, first_direction, second.T, second_direction.T)
    return grad_a, grad_b.T


def solution(mesh):
    in_specs = (
        P("dp", None),
        P(("dp", "vocab"), None),
        P(),
        P(("dp", "vocab"), None),
        P(),
        P(("dp", "vocab"), None),
    )
    out_specs = (P(), P(("dp", "vocab"), None))
    return jax.shard_map(shards, mesh=mesh, in_specs=in_specs, out_specs=out_specs, check_vma=False)
```

```python
import jax
import jax.numpy as jnp
from jax import lax
from jax.experimental import pallas as pl
from jax.experimental.pallas import tpu as pltpu
from jax.sharding import PartitionSpec as P

MESH = pl.DeviceIdType.MESH
F32 = jnp.float32
BF16 = jnp.bfloat16

WIDTH = 4608
RANK = 64
VOCAB = 768
TOKENS = 1024
CHUNK = 256
ROWS = VOCAB + 2 * RANK
NX, NY, NZ = 4, 4, 8
HALF = 2304
PART = 64
BLOCK = 64
COLS = 512


def place(x, y, z, c):
    return (y, x * 16 + z * 2 + c)


def remote(src, dst, send_sem, recv_sem, device):
    return pltpu.make_async_remote_copy(
        src_ref=src,
        dst_ref=dst,
        send_sem=send_sem,
        recv_sem=recv_sem,
        device_id=device,
        device_id_type=MESH,
    )


def merge(parts):
    top = parts[0][0]
    for part in parts[1:]:
        top = jnp.maximum(top, part[0])
    scales = [jnp.exp(part[0] - top) for part in parts]
    total = scales[0] * parts[0][1]
    weighted = total * parts[0][2]
    for scale, part in zip(scales[1:], parts[1:]):
        share = scale * part[1]
        total = total + share
        weighted = weighted + share * part[2]
    mean = weighted / total
    moved = None
    plain = None
    for scale, part in zip(scales, parts):
        shift = scale * (part[2] - mean)
        one = scale * part[3] + shift * part[4]
        two = scale * part[4]
        moved = one if moved is None else moved + one
        plain = two if plain is None else plain + two
    return top, total, mean, moved, plain


def stat_rows(top, total, mean):
    return jnp.concatenate([top, total, mean, jnp.zeros((5, top.shape[1]), F32)], axis=0)


def kernel(
    s_ref, w_ref, a_ref, ad_ref, bt_hbm, dbt_hbm, ga_ref, gb_ref,
    bt_ref, dbt_ref,
    wall, sg, acc, e_buf, t_buf, xr, bl, bt2, h1, h2, hs,
    p0, r1, p1, r2, r3, cg, stg,
    load_sem, ys, yr, ns, nr, gs, gr, ss1, sr1, xs, xrv, zs, zr, cs, cr, ts, tr, fs, fr,
):
    y = lax.axis_index("dp")
    v = lax.axis_index("vocab")
    x, z, c = v // 16, (v // 2) % 8, v % 2
    sib = place(x, y, z, 1 - c)
    y_up, y_down = place(x, (y + 1) % NY, z, c), place(x, (y + 3) % NY, z, c)
    pairs = [(dx, dy) for dx in range(NX) for dy in range(NY) if (dx, dy) != (0, 0)]
    xy = [((x + dx) % NX, (y + dy) % NY) for dx, dy in pairs]

    barrier = pltpu.get_barrier_semaphore()
    everyone = [sib] + [place(px, py, z, c) for px, py in xy] + [place(x, y, (z + d) % NZ, c) for d in range(1, NZ)]
    for peer in everyone:
        pl.semaphore_signal(barrier, 1, device_id=peer, device_id_type=MESH)

    def rows_of(j, start, size):
        return sg.at[pl.ds(pl.multiple_of(j * CHUNK + start, 16), size)]

    loads = [
        pltpu.make_async_copy(s_ref, rows_of(y, 0, CHUNK), load_sem.at[0]),
        pltpu.make_async_copy(w_ref, wall.at[pl.ds(0, VOCAB)], load_sem.at[1]),
        pltpu.make_async_copy(a_ref, wall.at[pl.ds(VOCAB, RANK)], load_sem.at[2]),
        pltpu.make_async_copy(ad_ref, wall.at[pl.ds(VOCAB + RANK, RANK)], load_sem.at[3]),
        pltpu.make_async_copy(bt_hbm, bt_ref, load_sem.at[4]),
        pltpu.make_async_copy(dbt_hbm, dbt_ref, load_sem.at[5]),
    ]
    for load in loads:
        load.start()

    pl.semaphore_wait(barrier, len(everyone))

    colour = (x + z) % 2
    before, after, across = (y + 3) % NY, (y + 1) % NY, (y + 2) % NY
    steps = [(before, 0), (after, 1), (before, 1), (after, 0), (across, 0), (across, 1)]
    around = [
        place((x + 1) % NX, y, z, c),
        place((x + 3) % NX, y, z, c),
        place(x, y, (z + 1) % NZ, c),
        place(x, y, (z + 7) % NZ, c),
    ]
    sends = []

    def send(make):
        make().start()
        sends.append(make)

    def drain():
        for make in sends:
            make().wait_send()
        sends.clear()

    def arrived(ref, send_sem, recv_sem):
        remote(ref, ref, send_sem, recv_sem, sib).wait_recv()

    def piece(j, core, shade, h, first=0, size=PART):
        row = pl.multiple_of(j * CHUNK + (core * 2 + shade) * PART + first, 16)
        return sg.at[pl.ds(row, size), pl.ds(h * HALF, HALF)]

    def start_y(k, h, device):
        def make():
            row = pl.multiple_of((c * 2 + colour) * PART, 16)
            held = s_ref.at[pl.ds(row, PART), pl.ds(h * HALF, HALF)]
            return remote(held, piece(y, c, colour, h), ys.at[k], yr.at[k], device)

        send(make)

    def forward(pick, send_sems, recv_sems, n, device):
        send(lambda: remote(pick(), pick(), send_sems.at[n], recv_sems.at[n], device))

    def from_y(k):
        j, h = steps[k]

        def held():
            return piece(j, c, colour, h)

        arrived(held(), ys.at[k], yr.at[k])
        if k == 0:
            forward(held, ys, yr, 4, y_up)
        if k == 1:
            forward(held, ys, yr, 5, y_down)
        for i, device in enumerate(around):
            n = k * 4 + i
            forward(lambda i=i: piece(j, c, colour, h, 16 * i, 16), ns, nr, n, device)
        forward(held, gs, gr, k * 2, sib)

    def from_around(k):
        j, h = steps[k]
        for i in range(4):
            arrived(piece(j, c, 1 - colour, h, 16 * i, 16), ns.at[k * 4 + i], nr.at[k * 4 + i])
        forward(lambda: piece(j, c, 1 - colour, h), gs, gr, k * 2 + 1, sib)

    def from_sib(k):
        j, h = steps[k]
        arrived(piece(j, 1 - c, colour, h), gs.at[k * 2], gr.at[k * 2])
        arrived(piece(j, 1 - c, 1 - colour, h), gs.at[k * 2 + 1], gr.at[k * 2 + 1])

    start_y(0, 0, y_up)
    start_y(1, 1, y_down)
    start_y(2, 1, y_up)
    start_y(3, 0, y_down)

    def finish(j, acc):
        first = pl.multiple_of(j * CHUNK, CHUNK)
        here = pl.ds(first, CHUNK)

        low = acc[VOCAB:ROWS, :].astype(BF16)
        xr[:, here] = low
        e_buf[:, here] = acc[0:VOCAB, :] + jnp.dot(bl[...], low, preferred_element_type=F32)
        t_buf[:, here] = jnp.dot(bt2[...], low, preferred_element_type=F32)
        blocks = [pl.ds(i, BLOCK) for i in range(0, VOCAB, BLOCK)]

        def fold(values, add):
            return add(values.reshape(BLOCK // 8, 8, CHUNK), axis=0)

        top = fold(e_buf[blocks[0], here], jnp.max)
        for at in blocks[1:]:
            top = jnp.maximum(top, fold(e_buf[at, here], jnp.max))
        top = jnp.max(top, axis=0, keepdims=True)
        total = jnp.zeros((8, CHUNK), F32)
        weighted = jnp.zeros((8, CHUNK), F32)
        for at in blocks:
            e = jnp.exp(e_buf[at, here] - top)
            e_buf[at, here] = e
            h2[at, :] = e.astype(BF16)
            total = total + fold(e, jnp.sum)
            weighted = weighted + fold(e * t_buf[at, here], jnp.sum)
        total = jnp.sum(total, axis=0, keepdims=True)
        mean = jnp.sum(weighted, axis=0, keepdims=True) / total
        for at in blocks:
            h1[at, :] = (e_buf[at, here] * (t_buf[at, here] - mean)).astype(BF16)
        side, there = j // 2, pl.ds(pl.multiple_of((j % 2) * CHUNK, CHUNK), CHUNK)
        p0[side, 0:RANK, there] = jnp.dot(bt_ref[...], h1[...], preferred_element_type=F32)
        p0[side, RANK : 2 * RANK, there] = jnp.dot(bt_ref[...], h2[...], preferred_element_type=F32)
        p0[side, 2 * RANK : 2 * RANK + 8, there] = stat_rows(top, total, mean)

    for load in loads:
        load.wait()
    bt = bt_ref[...].astype(F32)
    dbt = dbt_ref[...].astype(F32)
    bl[...] = jnp.concatenate([bt, jnp.zeros_like(bt)], axis=0).T.astype(BF16)
    bt2[...] = jnp.concatenate([dbt, bt], axis=0).T.astype(BF16)

    def any_of(i, *values):
        hit = i == values[0]
        for value in values[1:]:
            hit = hit | (i == value)
        return hit

    def work(i, carry):
        @pl.when(i == 2)
        def _():
            from_y(0)
            from_y(1)
            from_around(0)
            from_around(1)
            from_y(2)
            from_y(3)
            from_sib(0)

        @pl.when(i == 3)
        def _():
            from_sib(1)

        @pl.when(i == 4)
        def _():
            from_around(2)
            from_around(3)
            from_y(4)
            from_y(5)
            from_sib(2)

        @pl.when(i == 5)
        def _():
            from_sib(3)

        @pl.when(i == 6)
        def _():
            from_sib(4)

        @pl.when(i == 7)
        def _():
            from_sib(5)

        step = jnp.where(i < 2, 0, jnp.where(any_of(i, 2, 4), 3, jnp.where(i < 6, 1, 2)))
        j = (y + step) % NY
        h = jnp.where(any_of(i, 1, 3, 4, 7), 1, 0)
        total = acc.at[jnp.where(step == 1, 1, 0)]
        here = pl.ds(pl.multiple_of(j * CHUNK, CHUNK), CHUNK)
        at = pl.ds(pl.multiple_of(h * HALF, 128), HALF)
        part = lax.dot_general(wall[:, at], sg[here, at], (((1,), (1,)), ((), ())), preferred_element_type=F32)
        fresh = any_of(i, 0, 2, 3, 6)

        @pl.when(fresh)
        def _():
            total[...] = part

        @pl.when(jnp.logical_not(fresh))
        def _():
            total[...] += part

        @pl.when(i == 5)
        def _():
            from_around(4)
            from_around(5)

        @pl.when(any_of(i, 1, 4, 5, 7))
        def _():
            finish(j, total)

        return carry

    lax.fori_loop(0, 8, work, 0)

    send(lambda: remote(p0.at[1 - c], r1, ss1.at[0], sr1.at[0], sib))
    arrived(r1, ss1.at[0], sr1.at[0])
    for tx in range(NX):
        lanes = pl.ds(tx * 128, 128)

        def stats(ref, row):
            return ref[pl.ds(row, 1), lanes]

        own, other = p0.at[c], r1
        for ty in range(NY):
            g1, g2 = pl.ds(ty * 16, 16), pl.ds(RANK + ty * 16, 16)
            out = merge(
                [
                    (stats(ref, 128), stats(ref, 129), stats(ref, 130), ref[g1, lanes], ref[g2, lanes])
                    for ref in (own, other)
                ]
            )
            p1[tx * NY + ty] = jnp.concatenate([out[3], out[4], stat_rows(*out[:3])], axis=0)

    def unpack(ref, k):
        return (ref[k, 32:33], ref[k, 33:34], ref[k, 34:35], ref[k, 0:16], ref[k, 16:32])

    me = x * NY + y
    early = list(sends)
    sends.clear()
    for k, (px, py) in enumerate(xy):
        send(
            lambda k=k, px=px, py=py: remote(
                p1.at[px * NY + py], r2.at[me], xs.at[k], xrv.at[k], place(px, py, z, c)
            )
        )
    for make in early:
        make().wait_send()
    r2[me] = p1[me]
    for k, (dx, dy) in enumerate(pairs):
        origin = ((x - dx + NX) % NX) * NY + (y - dy + NY) % NY
        arrived(r2.at[origin], xs.at[k], xrv.at[k])
    out = merge([unpack(r2, k) for k in range(NX * NY)])
    r3[z] = jnp.concatenate([out[3], out[4], stat_rows(*out[:3])], axis=0)
    for d in range(1, NZ):
        forward(lambda: r3.at[z], zs, zr, d - 1, place(x, y, (z + d) % NZ, c))
    for d in range(1, NZ):
        arrived(r3.at[(z - d + NZ) % NZ], zs.at[d - 1], zr.at[d - 1])
    top, total, mean, moved, plain = merge([unpack(r3, k) for k in range(NZ)])

    slot = c * NX + x
    strip = cg.at[slot, pl.ds(pl.multiple_of(y * 16, 16), 16)]
    strip[...] = (moved / total).astype(BF16)
    stg[slot] = stat_rows(top, total, mean)
    for d in range(1, NX):
        forward(lambda: stg.at[slot], ts, tr, d - 1, place((x + d) % NX, y, z, c))
    for k, (px, py) in enumerate(xy):
        forward(lambda: strip, cs, cr, k, place(px, py, z, c))
    for d in range(1, NX):
        arrived(stg.at[c * NX + (x - d + NX) % NX], ts.at[d - 1], tr.at[d - 1])
    forward(lambda: stg.at[pl.ds(c * NX, NX)], fs, fr, 0, sib)
    for k, (dx, dy) in enumerate(pairs):
        from_x, from_y = (x - dx + NX) % NX, (y - dy + NY) % NY
        arrived(cg.at[c * NX + from_x, pl.ds(pl.multiple_of(from_y * 16, 16), 16)], cs.at[k], cr.at[k])
    forward(lambda: cg.at[pl.ds(c * NX, NX)], fs, fr, 1, sib)
    arrived(stg.at[pl.ds((1 - c) * NX, NX)], fs.at[0], fr.at[0])

    factors, means = [], []
    for t in range(8):
        local_top = p0[t // 4, 128:129, (t % 4) * 128 : (t % 4 + 1) * 128]
        factors.append(jnp.exp(local_top - stg[t, 0:1]) / stg[t, 1:2])
        means.append(stg[t, 2:3])

    def hessian(i, carry):
        at = pl.ds(pl.multiple_of(i * BLOCK, BLOCK), BLOCK)
        for t in range(8):
            lanes = pl.ds(t * 128, 128)
            probs = e_buf[at, lanes] * factors[t]
            hs[at, lanes] = (probs * (t_buf[at, lanes] - means[t])).astype(BF16)
        return carry

    lax.fori_loop(0, VOCAB // BLOCK, hessian, 0)
    gb_ref[...] = lax.dot_general(xr[0:RANK, :], hs[...], (((1,), (1,)), ((), ())), preferred_element_type=F32)

    def outer(core, first):
        rows = pl.ds(pl.multiple_of(core * (TOKENS // 2), TOKENS // 2), TOKENS // 2)
        lows = jnp.concatenate([cg[core * NX + t] for t in range(NX)], axis=1)

        def columns(n, carry):
            at = pl.ds(pl.multiple_of(n * COLS, 128), COLS)
            part = jnp.dot(lows, sg[rows, at], preferred_element_type=F32)
            ga_ref[:, at] = part if first else ga_ref[:, at] + part
            return carry

        lax.fori_loop(0, WIDTH // COLS, columns, 0)

    outer(c, True)
    arrived(cg.at[pl.ds((1 - c) * NX, NX)], fs.at[1], fr.at[1])
    outer(1 - c, False)
    drain()


def shards(states, weight, first, second, first_direction, second_direction):
    vmem = pl.BlockSpec(memory_space=pltpu.VMEM)
    hbm = pl.BlockSpec(memory_space=pl.ANY)
    dma = pltpu.SemaphoreType.DMA
    grad_a, grad_b = pl.pallas_call(
        kernel,
        out_shape=(pltpu.VMEM((RANK, WIDTH), F32), pltpu.VMEM((RANK, VOCAB), F32)),
        in_specs=[hbm] * 6,
        out_specs=(vmem, vmem),
        scratch_shapes=[
            pltpu.VMEM((RANK, VOCAB), BF16),
            pltpu.VMEM((RANK, VOCAB), BF16),
            pltpu.VMEM((ROWS, WIDTH), BF16),
            pltpu.VMEM((TOKENS, WIDTH), BF16),
            pltpu.VMEM((2, ROWS, CHUNK), F32),
            pltpu.VMEM((VOCAB, TOKENS), F32),
            pltpu.VMEM((VOCAB, TOKENS), F32),
            pltpu.VMEM((2 * RANK, TOKENS), BF16),
            pltpu.VMEM((VOCAB, 2 * RANK), BF16),
            pltpu.VMEM((VOCAB, 2 * RANK), BF16),
            pltpu.VMEM((VOCAB, CHUNK), BF16),
            pltpu.VMEM((VOCAB, CHUNK), BF16),
            pltpu.VMEM((VOCAB, TOKENS), BF16),
            pltpu.VMEM((2, 2 * RANK + 8, TOKENS // 2), F32),
            pltpu.VMEM((2 * RANK + 8, TOKENS // 2), F32),
            pltpu.VMEM((NX * NY, 40, 128), F32),
            pltpu.VMEM((NX * NY, 40, 128), F32),
            pltpu.VMEM((NZ, 40, 128), F32),
            pltpu.VMEM((2 * NX, RANK, 128), BF16),
            pltpu.VMEM((2 * NX, 8, 128), F32),
            dma((6,)),
            dma((6,)), dma((6,)),
            dma((24,)), dma((24,)),
            dma((12,)), dma((12,)),
            dma((1,)), dma((1,)),
            dma((15,)), dma((15,)),
            dma((7,)), dma((7,)),
            dma((15,)), dma((15,)),
            dma((3,)), dma((3,)),
            dma((2,)), dma((2,)),
        ],
        compiler_params=pltpu.CompilerParams(
            collective_id=0, has_side_effects=True, vmem_limit_bytes=56 * 1024 * 1024
        ),
        cost_estimate=pl.CostEstimate(flops=10_000_000_000, bytes_accessed=20_000_000, transcendentals=800_000),
    )(states, weight, first, first_direction, second.T, second_direction.T)
    return grad_a, grad_b.T


def solution(mesh):
    in_specs = (
        P("dp", None),
        P(("dp", "vocab"), None),
        P(),
        P(("dp", "vocab"), None),
        P(),
        P(("dp", "vocab"), None),
    )
    out_specs = (P(), P(("dp", "vocab"), None))
    return jax.shard_map(shards, mesh=mesh, in_specs=in_specs, out_specs=out_specs, check_vma=False)
```

```python
import jax
import jax.numpy as jnp
from jax import lax
from jax.experimental import pallas as pl
from jax.experimental.pallas import tpu as pltpu
from jax.sharding import PartitionSpec as P

MESH = pl.DeviceIdType.MESH
F32 = jnp.float32
BF16 = jnp.bfloat16

WIDTH = 4608
RANK = 64
VOCAB = 768
TOKENS = 1024
CHUNK = 256
ROWS = VOCAB + 2 * RANK
NX, NY, NZ = 4, 4, 8
HALF = 2304
QUARTER = 1152
BLOCK = 64
COLS = 512


def place(x, y, z, c):
    return (y, x * 16 + z * 2 + c)


def remote(src, dst, send_sem, recv_sem, device):
    return pltpu.make_async_remote_copy(
        src_ref=src,
        dst_ref=dst,
        send_sem=send_sem,
        recv_sem=recv_sem,
        device_id=device,
        device_id_type=MESH,
    )


def merge(parts):
    top = parts[0][0]
    for part in parts[1:]:
        top = jnp.maximum(top, part[0])
    scales = [jnp.exp(part[0] - top) for part in parts]
    total = scales[0] * parts[0][1]
    weighted = total * parts[0][2]
    for scale, part in zip(scales[1:], parts[1:]):
        share = scale * part[1]
        total = total + share
        weighted = weighted + share * part[2]
    mean = weighted / total
    moved = None
    plain = None
    for scale, part in zip(scales, parts):
        shift = scale * (part[2] - mean)
        one = scale * part[3] + shift * part[4]
        two = scale * part[4]
        moved = one if moved is None else moved + one
        plain = two if plain is None else plain + two
    return top, total, mean, moved, plain


def stat_rows(top, total, mean):
    return jnp.concatenate([top, total, mean, jnp.zeros((5, top.shape[1]), F32)], axis=0)


def kernel(
    s_ref, w_ref, a_ref, ad_ref, bt_hbm, dbt_hbm, ga_ref, gb_ref,
    bt_ref, dbt_ref,
    wall, sg, acc, e_buf, t_buf, xr, bl, bt2, h1, h2, hs,
    p0, r1, p1, r2, r3, cg, stg,
    load_sem, ys, yr, ns, nr, gs, gr, ss1, sr1, xs, xrv, zs, zr, cs, cr, ts, tr, fs, fr,
):
    y = lax.axis_index("dp")
    v = lax.axis_index("vocab")
    x, z, c = v // 16, (v // 2) % 8, v % 2
    sib = place(x, y, z, 1 - c)
    y_up, y_down = place(x, (y + 1) % NY, z, c), place(x, (y + 3) % NY, z, c)
    pairs = [(dx, dy) for dx in range(NX) for dy in range(NY) if (dx, dy) != (0, 0)]
    xy = [((x + dx) % NX, (y + dy) % NY) for dx, dy in pairs]

    barrier = pltpu.get_barrier_semaphore()
    everyone = [sib] + [place(px, py, z, c) for px, py in xy] + [place(x, y, (z + d) % NZ, c) for d in range(1, NZ)]
    everyone += [place((x + dx) % NX, y, (z + dz) % NZ, c) for dx in (1, 3) for dz in (1, 7)]
    for peer in everyone:
        pl.semaphore_signal(barrier, 1, device_id=peer, device_id_type=MESH)

    def rows_of(j, start, size):
        return sg.at[pl.ds(pl.multiple_of(j * CHUNK + start, 16), size)]

    loads = [
        pltpu.make_async_copy(s_ref, rows_of(y, 0, CHUNK), load_sem.at[0]),
        pltpu.make_async_copy(w_ref, wall.at[pl.ds(0, VOCAB)], load_sem.at[1]),
        pltpu.make_async_copy(a_ref, wall.at[pl.ds(VOCAB, RANK)], load_sem.at[2]),
        pltpu.make_async_copy(ad_ref, wall.at[pl.ds(VOCAB + RANK, RANK)], load_sem.at[3]),
        pltpu.make_async_copy(bt_hbm, bt_ref, load_sem.at[4]),
        pltpu.make_async_copy(dbt_hbm, dbt_ref, load_sem.at[5]),
    ]
    for load in loads:
        load.start()

    pl.semaphore_wait(barrier, len(everyone))

    odd = x % 2
    colour = (x + z) % 2
    lead, rest, wide = colour * 64 + odd * 32, colour * 64 + 32 - odd * 16, colour * 64 + 32 - odd * 32
    corner, missing = colour * 64 + odd * 48, colour * 64 + (1 - odd) * 48
    other = (1 - colour) * 64
    other_x, other_z = other + (1 - odd) * 32, other + odd * 32
    before, after, across = (y + 3) % NY, (y + 1) % NY, (y + 2) % NY
    whole = (2, 3)
    steps = [(before, 0), (after, 1), (before, 1), (after, 0), (across, 0), (across, 1)]
    around = [
        place((x + 1) % NX, y, z, c),
        place((x + 3) % NX, y, z, c),
        place(x, y, (z + 1) % NZ, c),
        place(x, y, (z + 7) % NZ, c),
    ]
    corners = [
        [place((x + 1) % NX, y, (z + 1) % NZ, c), place((x + 3) % NX, y, (z + 7) % NZ, c)],
        [place((x + 1) % NX, y, (z + 7) % NZ, c), place((x + 3) % NX, y, (z + 1) % NZ, c)],
    ]
    sends = []

    def send(make):
        make().start()
        sends.append(make)

    def drain():
        for make in sends:
            make().wait_send()
        sends.clear()

    def arrived(ref, send_sem, recv_sem):
        remote(ref, ref, send_sem, recv_sem, sib).wait_recv()

    def piece(j, core, first, size, column, width=HALF):
        row = pl.multiple_of(j * CHUNK + core * (CHUNK // 2) + first, 16)
        return sg.at[pl.ds(row, size), pl.ds(column, width)]

    def start_y(k, h, first, size, device):
        def make():
            row = pl.multiple_of(c * (CHUNK // 2) + first, 16)
            held = s_ref.at[pl.ds(row, size), pl.ds(h * HALF, HALF)]
            return remote(held, piece(y, c, first, size, h * HALF), ys.at[k], yr.at[k], device)

        send(make)

    def forward(pick, send_sems, recv_sems, n, device):
        send(lambda: remote(pick(), pick(), send_sems.at[n], recv_sems.at[n], device))

    def from_y(k):
        j, h = steps[k]
        left = h * HALF

        def held():
            return piece(j, c, lead, 32, left)

        arrived(held(), ys.at[k], yr.at[k])
        for i, device in enumerate(around):
            column = left + (i % 2) * QUARTER
            forward(lambda column=column: piece(j, c, lead, 32, column, QUARTER), ns, nr, k * 6 + i, device)
        for i, device in enumerate([] if k in whole else corners[h]):
            column = left + i * QUARTER
            forward(lambda column=column: piece(j, c, corner, 16, column, QUARTER), ns, nr, k * 6 + 4 + i, device)
        if k < 2:
            forward(held, ys, yr, k + 4, (y_up, y_down)[k])
        forward(held, gs, gr, k * 4, sib)

    def rest_y(k):
        j, h = steps[k]

        def held():
            return piece(j, c, wide, 32, h * HALF) if k in whole else piece(j, c, rest, 16, h * HALF)

        arrived(held(), ys.at[k + 6], yr.at[k + 6])
        if k < 2:
            forward(held, ys, yr, k + 10, (y_up, y_down)[k])
        forward(held, gs, gr, k * 4 + 3, sib)

    def from_around(k):
        j, h = steps[k]
        left = h * HALF
        for i in range(4):
            first = other_x if i < 2 else other_z
            n = k * 6 + i
            arrived(piece(j, c, first, 32, left + (i % 2) * QUARTER, QUARTER), ns.at[n], nr.at[n])
        forward(lambda: piece(j, c, other, 64, left), gs, gr, k * 4 + 1, sib)
        if k in whole:
            return
        for i in range(2):
            n = k * 6 + 4 + i
            arrived(piece(j, c, missing, 16, left + i * QUARTER, QUARTER), ns.at[n], nr.at[n])
        forward(lambda: piece(j, c, missing, 16, left), gs, gr, k * 4 + 2, sib)

    def from_sib(k):
        j, h = steps[k]
        parts = [(0, lead, 32), (1, other, 64)]
        parts += [(3, wide, 32)] if k in whole else [(2, missing, 16), (3, rest, 16)]
        for i, first, size in parts:
            arrived(piece(j, 1 - c, first, size, h * HALF), gs.at[k * 4 + i], gr.at[k * 4 + i])

    for k, (h, device) in enumerate([(0, y_up), (1, y_down), (1, y_up), (0, y_down)]):
        start_y(k, h, lead, 32, device)
    for k, (h, device) in enumerate([(0, y_up), (1, y_down)]):
        start_y(6 + k, h, rest, 16, device)

    def finish(j, acc):
        first = pl.multiple_of(j * CHUNK, CHUNK)
        here = pl.ds(first, CHUNK)

        low = acc[VOCAB:ROWS, :].astype(BF16)
        xr[:, here] = low
        e_buf[:, here] = acc[0:VOCAB, :] + jnp.dot(bl[...], low, preferred_element_type=F32)
        t_buf[:, here] = jnp.dot(bt2[...], low, preferred_element_type=F32)
        blocks = [pl.ds(i, BLOCK) for i in range(0, VOCAB, BLOCK)]

        def fold(values, add):
            return add(values.reshape(BLOCK // 8, 8, CHUNK), axis=0)

        top = fold(e_buf[blocks[0], here], jnp.max)
        for at in blocks[1:]:
            top = jnp.maximum(top, fold(e_buf[at, here], jnp.max))
        top = jnp.max(top, axis=0, keepdims=True)
        total = jnp.zeros((8, CHUNK), F32)
        weighted = jnp.zeros((8, CHUNK), F32)
        for at in blocks:
            e = jnp.exp(e_buf[at, here] - top)
            e_buf[at, here] = e
            h2[at, :] = e.astype(BF16)
            total = total + fold(e, jnp.sum)
            weighted = weighted + fold(e * t_buf[at, here], jnp.sum)
        total = jnp.sum(total, axis=0, keepdims=True)
        mean = jnp.sum(weighted, axis=0, keepdims=True) / total
        for at in blocks:
            h1[at, :] = (e_buf[at, here] * (t_buf[at, here] - mean)).astype(BF16)
        side, there = j // 2, pl.ds(pl.multiple_of((j % 2) * CHUNK, CHUNK), CHUNK)
        p0[side, 0:RANK, there] = jnp.dot(bt_ref[...], h1[...], preferred_element_type=F32)
        p0[side, RANK : 2 * RANK, there] = jnp.dot(bt_ref[...], h2[...], preferred_element_type=F32)
        p0[side, 2 * RANK : 2 * RANK + 8, there] = stat_rows(top, total, mean)

    for load in loads:
        load.wait()
    bt = bt_ref[...].astype(F32)
    dbt = dbt_ref[...].astype(F32)
    bl[...] = jnp.concatenate([bt, jnp.zeros_like(bt)], axis=0).T.astype(BF16)
    bt2[...] = jnp.concatenate([dbt, bt], axis=0).T.astype(BF16)

    def any_of(i, *values):
        hit = i == values[0]
        for value in values[1:]:
            hit = hit | (i == value)
        return hit

    def work(i, carry):
        @pl.when(i == 1)
        def _():
            from_y(0)
            from_y(1)
            start_y(8, 1, wide, 32, y_up)
            start_y(9, 0, wide, 32, y_down)

        @pl.when(i == 2)
        def _():
            from_y(2)
            from_y(3)
            rest_y(0)
            rest_y(1)
            from_around(0)
            from_around(1)
            from_y(4)
            from_y(5)
            from_sib(0)

        @pl.when(i == 3)
        def _():
            from_sib(1)

        @pl.when(i == 4)
        def _():
            rest_y(2)
            rest_y(3)
            from_around(2)
            from_around(3)
            from_sib(2)

        @pl.when(i == 5)
        def _():
            from_sib(3)

        @pl.when(i == 6)
        def _():
            from_sib(4)

        @pl.when(i == 7)
        def _():
            from_sib(5)

        step = jnp.where(i < 2, 0, jnp.where(any_of(i, 2, 4), 3, jnp.where(i < 6, 1, 2)))
        j = (y + step) % NY
        h = jnp.where(any_of(i, 1, 3, 4, 7), 1, 0)
        total = acc.at[jnp.where(step == 1, 1, 0)]
        here = pl.ds(pl.multiple_of(j * CHUNK, CHUNK), CHUNK)
        at = pl.ds(pl.multiple_of(h * HALF, 128), HALF)
        part = lax.dot_general(wall[:, at], sg[here, at], (((1,), (1,)), ((), ())), preferred_element_type=F32)
        fresh = any_of(i, 0, 2, 3, 6)

        @pl.when(fresh)
        def _():
            total[...] = part

        @pl.when(jnp.logical_not(fresh))
        def _():
            total[...] += part

        @pl.when(i == 4)
        def _():
            rest_y(4)
            rest_y(5)
            from_around(4)

        @pl.when(i == 5)
        def _():
            from_around(5)

        @pl.when(any_of(i, 1, 4, 5, 7))
        def _():
            finish(j, total)

        return carry

    lax.fori_loop(0, 8, work, 0)

    send(lambda: remote(p0.at[1 - c], r1, ss1.at[0], sr1.at[0], sib))
    arrived(r1, ss1.at[0], sr1.at[0])
    for tx in range(NX):
        lanes = pl.ds(tx * 128, 128)

        def stats(ref, row):
            return ref[pl.ds(row, 1), lanes]

        ours, theirs = p0.at[c], r1
        for ty in range(NY):
            g1, g2 = pl.ds(ty * 16, 16), pl.ds(RANK + ty * 16, 16)
            out = merge(
                [
                    (stats(ref, 128), stats(ref, 129), stats(ref, 130), ref[g1, lanes], ref[g2, lanes])
                    for ref in (ours, theirs)
                ]
            )
            p1[tx * NY + ty] = jnp.concatenate([out[3], out[4], stat_rows(*out[:3])], axis=0)

    def unpack(ref, k):
        return (ref[k, 32:33], ref[k, 33:34], ref[k, 34:35], ref[k, 0:16], ref[k, 16:32])

    me = x * NY + y
    early = list(sends)
    sends.clear()
    for k, (px, py) in enumerate(xy):
        send(
            lambda k=k, px=px, py=py: remote(
                p1.at[px * NY + py], r2.at[me], xs.at[k], xrv.at[k], place(px, py, z, c)
            )
        )
    for make in early:
        make().wait_send()
    r2[me] = p1[me]
    for k, (dx, dy) in enumerate(pairs):
        origin = ((x - dx + NX) % NX) * NY + (y - dy + NY) % NY
        arrived(r2.at[origin], xs.at[k], xrv.at[k])
    out = merge([unpack(r2, k) for k in range(NX * NY)])
    r3[z] = jnp.concatenate([out[3], out[4], stat_rows(*out[:3])], axis=0)
    for d in range(1, NZ):
        forward(lambda: r3.at[z], zs, zr, d - 1, place(x, y, (z + d) % NZ, c))
    for d in range(1, NZ):
        arrived(r3.at[(z - d + NZ) % NZ], zs.at[d - 1], zr.at[d - 1])
    top, total, mean, moved, plain = merge([unpack(r3, k) for k in range(NZ)])

    slot = c * NX + x
    strip = cg.at[slot, pl.ds(pl.multiple_of(y * 16, 16), 16)]
    strip[...] = (moved / total).astype(BF16)
    stg[slot] = stat_rows(top, total, mean)
    for d in range(1, NX):
        forward(lambda: stg.at[slot], ts, tr, d - 1, place((x + d) % NX, y, z, c))
    for k, (px, py) in enumerate(xy):
        forward(lambda: strip, cs, cr, k, place(px, py, z, c))
    for d in range(1, NX):
        arrived(stg.at[c * NX + (x - d + NX) % NX], ts.at[d - 1], tr.at[d - 1])
    forward(lambda: stg.at[pl.ds(c * NX, NX)], fs, fr, 0, sib)

    def curve(core, first):
        tiles = [(pl.ds(pl.multiple_of(core * 512 + t * 128, 128), 128), core * NX + t) for t in range(NX)]
        factors, means = [], []
        for t, (lanes, k) in enumerate(tiles):
            local_top = p0[core, 2 * RANK : 2 * RANK + 1, t * 128 : (t + 1) * 128]
            factors.append(jnp.exp(local_top - stg[k, 0:1]) / stg[k, 1:2])
            means.append(stg[k, 2:3])

        def hessian(i, carry):
            at = pl.ds(pl.multiple_of(i * BLOCK, BLOCK), BLOCK)
            for t, (lanes, k) in enumerate(tiles):
                probs = e_buf[at, lanes] * factors[t]
                hs[at, lanes] = (probs * (t_buf[at, lanes] - means[t])).astype(BF16)
            return carry

        lax.fori_loop(0, VOCAB // BLOCK, hessian, 0)
        at = pl.ds(pl.multiple_of(core * 512, 512), 512)
        part = lax.dot_general(xr[0:RANK, at], hs[:, at], (((1,), (1,)), ((), ())), preferred_element_type=F32)
        gb_ref[...] = part if first else gb_ref[...] + part

    curve(c, True)
    for k, (dx, dy) in enumerate(pairs):
        at_x, at_y = (x - dx + NX) % NX, (y - dy + NY) % NY
        arrived(cg.at[c * NX + at_x, pl.ds(pl.multiple_of(at_y * 16, 16), 16)], cs.at[k], cr.at[k])
    forward(lambda: cg.at[pl.ds(c * NX, NX)], fs, fr, 1, sib)
    arrived(stg.at[pl.ds((1 - c) * NX, NX)], fs.at[0], fr.at[0])
    curve(1 - c, False)

    def outer(core, first):
        rows = pl.ds(pl.multiple_of(core * (TOKENS // 2), TOKENS // 2), TOKENS // 2)
        lows = jnp.concatenate([cg[core * NX + t] for t in range(NX)], axis=1)

        def columns(n, carry):
            at = pl.ds(pl.multiple_of(n * COLS, 128), COLS)
            part = jnp.dot(lows, sg[rows, at], preferred_element_type=F32)
            ga_ref[:, at] = part if first else ga_ref[:, at] + part
            return carry

        lax.fori_loop(0, WIDTH // COLS, columns, 0)

    outer(c, True)
    arrived(cg.at[pl.ds((1 - c) * NX, NX)], fs.at[1], fr.at[1])
    outer(1 - c, False)
    drain()


def shards(states, weight, first, second, first_direction, second_direction):
    vmem = pl.BlockSpec(memory_space=pltpu.VMEM)
    hbm = pl.BlockSpec(memory_space=pl.ANY)
    dma = pltpu.SemaphoreType.DMA
    grad_a, grad_b = pl.pallas_call(
        kernel,
        out_shape=(pltpu.VMEM((RANK, WIDTH), F32), pltpu.VMEM((RANK, VOCAB), F32)),
        in_specs=[hbm] * 6,
        out_specs=(vmem, vmem),
        scratch_shapes=[
            pltpu.VMEM((RANK, VOCAB), BF16),
            pltpu.VMEM((RANK, VOCAB), BF16),
            pltpu.VMEM((ROWS, WIDTH), BF16),
            pltpu.VMEM((TOKENS, WIDTH), BF16),
            pltpu.VMEM((2, ROWS, CHUNK), F32),
            pltpu.VMEM((VOCAB, TOKENS), F32),
            pltpu.VMEM((VOCAB, TOKENS), F32),
            pltpu.VMEM((2 * RANK, TOKENS), BF16),
            pltpu.VMEM((VOCAB, 2 * RANK), BF16),
            pltpu.VMEM((VOCAB, 2 * RANK), BF16),
            pltpu.VMEM((VOCAB, CHUNK), BF16),
            pltpu.VMEM((VOCAB, CHUNK), BF16),
            pltpu.VMEM((VOCAB, TOKENS), BF16),
            pltpu.VMEM((2, 2 * RANK + 8, TOKENS // 2), F32),
            pltpu.VMEM((2 * RANK + 8, TOKENS // 2), F32),
            pltpu.VMEM((NX * NY, 40, 128), F32),
            pltpu.VMEM((NX * NY, 40, 128), F32),
            pltpu.VMEM((NZ, 40, 128), F32),
            pltpu.VMEM((2 * NX, RANK, 128), BF16),
            pltpu.VMEM((2 * NX, 8, 128), F32),
            dma((6,)),
            dma((12,)), dma((12,)),
            dma((36,)), dma((36,)),
            dma((24,)), dma((24,)),
            dma((1,)), dma((1,)),
            dma((15,)), dma((15,)),
            dma((7,)), dma((7,)),
            dma((15,)), dma((15,)),
            dma((3,)), dma((3,)),
            dma((2,)), dma((2,)),
        ],
        compiler_params=pltpu.CompilerParams(
            collective_id=0, has_side_effects=True, vmem_limit_bytes=56 * 1024 * 1024
        ),
        cost_estimate=pl.CostEstimate(flops=10_000_000_000, bytes_accessed=20_000_000, transcendentals=800_000),
    )(states, weight, first, first_direction, second.T, second_direction.T)
    return grad_a, grad_b.T


def solution(mesh):
    in_specs = (
        P("dp", None),
        P(("dp", "vocab"), None),
        P(),
        P(("dp", "vocab"), None),
        P(),
        P(("dp", "vocab"), None),
    )
    out_specs = (P(), P(("dp", "vocab"), None))
    return jax.shard_map(shards, mesh=mesh, in_specs=in_specs, out_specs=out_specs, check_vma=False)
```

```python
import jax
import jax.numpy as jnp
from jax import lax
from jax.experimental import pallas as pl
from jax.experimental.pallas import tpu as pltpu
from jax.sharding import PartitionSpec as P

MESH = pl.DeviceIdType.MESH
F32 = jnp.float32
BF16 = jnp.bfloat16

WIDTH = 4608
RANK = 64
VOCAB = 768
TOKENS = 1024
CHUNK = 256
ROWS = VOCAB + 2 * RANK
NX, NY, NZ = 4, 4, 8
HALF = 2304
QUARTER = 1152
BLOCK = 64
COLS = 512


def place(x, y, z, c):
    return (y, x * 16 + z * 2 + c)


def remote(src, dst, send_sem, recv_sem, device):
    return pltpu.make_async_remote_copy(
        src_ref=src,
        dst_ref=dst,
        send_sem=send_sem,
        recv_sem=recv_sem,
        device_id=device,
        device_id_type=MESH,
    )


def merge(parts):
    top = parts[0][0]
    for part in parts[1:]:
        top = jnp.maximum(top, part[0])
    scales = [jnp.exp(part[0] - top) for part in parts]
    total = scales[0] * parts[0][1]
    weighted = total * parts[0][2]
    for scale, part in zip(scales[1:], parts[1:]):
        share = scale * part[1]
        total = total + share
        weighted = weighted + share * part[2]
    mean = weighted / total
    moved = None
    plain = None
    for scale, part in zip(scales, parts):
        shift = scale * (part[2] - mean)
        one = scale * part[3] + shift * part[4]
        two = scale * part[4]
        moved = one if moved is None else moved + one
        plain = two if plain is None else plain + two
    return top, total, mean, moved, plain


def stat_rows(top, total, mean):
    return jnp.concatenate([top, total, mean, jnp.zeros((5, top.shape[1]), F32)], axis=0)


def pack(top, total, mean, moved, plain):
    stats = jnp.concatenate([top, total, mean], axis=0)
    high = stats.astype(BF16).astype(F32)
    middle = (stats - high).astype(BF16).astype(F32)
    low = stats - high - middle
    blank = jnp.zeros((7, top.shape[1]), F32)
    return jnp.concatenate([moved, plain, high, middle, low, blank], axis=0).astype(BF16)


def unpack(ref, k):
    block = ref[k].astype(F32)
    stats = block[32:35] + block[35:38] + block[38:41]
    return stats[0:1], stats[1:2], stats[2:3], block[0:16], block[16:32]


def store(a_ref, b_ref, a_out, b_out, sems):
    copies = [
        pltpu.make_async_copy(a_ref, a_out, sems.at[0]),
        pltpu.make_async_copy(b_ref, b_out, sems.at[1]),
    ]
    for copy in copies:
        copy.start()
    for copy in copies:
        copy.wait()


def kernel(
    s_ref, w_ref, a_ref, ad_ref, bt_hbm, dbt_hbm, ga_ref, gb_ref,
    bt_ref, dbt_ref,
    wall, sg, acc, e_buf, t_buf, xr, bl, bt2, h1, h2, hs,
    p0, r1, p1, r2, r3, cg, stg,
    load_sem, ys, yr, ns, nr, gs, gr, ss1, sr1, xs, xrv, zs, zr, cs, cr, ts, tr, fs, fr,
):
    y = lax.axis_index("dp")
    v = lax.axis_index("vocab")
    x, z, c = v // 16, (v // 2) % 8, v % 2
    sib = place(x, y, z, 1 - c)
    y_up, y_down = place(x, (y + 1) % NY, z, c), place(x, (y + 3) % NY, z, c)
    pairs = [(dx, dy) for dx in range(NX) for dy in range(NY) if (dx, dy) != (0, 0)]
    xy = [((x + dx) % NX, (y + dy) % NY) for dx, dy in pairs]

    barrier = pltpu.get_barrier_semaphore()
    everyone = [y_up, y_down, sib]
    everyone += [place((x + dx) % NX, y, z, c) for dx in (1, 3)]
    everyone += [place(x, y, (z + d) % NZ, c) for d in range(1, NZ)]
    everyone += [place((x + dx) % NX, y, (z + dz) % NZ, c) for dx in (1, 3) for dz in (1, 7)]
    everyone += [place(px, py, z, c) for (dx, dy), (px, py) in zip(pairs, xy) if (dx, dy) not in ((0, 1), (0, 3), (1, 0), (3, 0))]
    for peer in everyone:
        pl.semaphore_signal(barrier, 1, device_id=peer, device_id_type=MESH)

    def rows_of(j, start, size):
        return sg.at[pl.ds(pl.multiple_of(j * CHUNK + start, 16), size)]

    loads = [
        pltpu.make_async_copy(s_ref, rows_of(y, 0, CHUNK), load_sem.at[0]),
        pltpu.make_async_copy(w_ref, wall.at[pl.ds(0, VOCAB)], load_sem.at[1]),
        pltpu.make_async_copy(a_ref, wall.at[pl.ds(VOCAB, RANK)], load_sem.at[2]),
        pltpu.make_async_copy(ad_ref, wall.at[pl.ds(VOCAB + RANK, RANK)], load_sem.at[3]),
        pltpu.make_async_copy(bt_hbm, bt_ref, load_sem.at[4]),
        pltpu.make_async_copy(dbt_hbm, dbt_ref, load_sem.at[5]),
    ]
    for load in loads:
        load.start()

    pl.semaphore_wait(barrier, len(everyone))

    odd = x % 2
    colour = (x + z) % 2
    lead, rest, wide = colour * 64 + odd * 32, colour * 64 + 32 - odd * 16, colour * 64 + 32 - odd * 32
    corner, missing = colour * 64 + odd * 48, colour * 64 + (1 - odd) * 48
    other = (1 - colour) * 64
    other_x, other_z = other + (1 - odd) * 32, other + odd * 32
    before, after, across = (y + 3) % NY, (y + 1) % NY, (y + 2) % NY
    whole = (2, 3)
    steps = [(before, 0), (after, 1), (before, 1), (after, 0), (across, 0), (across, 1)]
    around = [
        place((x + 1) % NX, y, z, c),
        place((x + 3) % NX, y, z, c),
        place(x, y, (z + 1) % NZ, c),
        place(x, y, (z + 7) % NZ, c),
    ]
    corners = [
        [place((x + 1) % NX, y, (z + 1) % NZ, c), place((x + 3) % NX, y, (z + 7) % NZ, c)],
        [place((x + 1) % NX, y, (z + 7) % NZ, c), place((x + 3) % NX, y, (z + 1) % NZ, c)],
    ]
    sends = []

    def send(make):
        make().start()
        sends.append(make)

    def drain():
        for make in sends:
            make().wait_send()
        sends.clear()

    def arrived(ref, send_sem, recv_sem):
        remote(ref, ref, send_sem, recv_sem, sib).wait_recv()

    def piece(j, core, first, size, column, width=HALF):
        row = pl.multiple_of(j * CHUNK + core * (CHUNK // 2) + first, 16)
        return sg.at[pl.ds(row, size), pl.ds(column, width)]

    def start_y(k, h, first, size, device):
        def make():
            row = pl.multiple_of(c * (CHUNK // 2) + first, 16)
            held = s_ref.at[pl.ds(row, size), pl.ds(h * HALF, HALF)]
            return remote(held, piece(y, c, first, size, h * HALF), ys.at[k], yr.at[k], device)

        send(make)

    def forward(pick, send_sems, recv_sems, n, device):
        send(lambda: remote(pick(), pick(), send_sems.at[n], recv_sems.at[n], device))

    def from_y(k):
        j, h = steps[k]
        left = h * HALF

        def held():
            return piece(j, c, lead, 32, left)

        arrived(held(), ys.at[k], yr.at[k])
        for i, device in enumerate(around):
            column = left + (i % 2) * QUARTER
            forward(lambda column=column: piece(j, c, lead, 32, column, QUARTER), ns, nr, k * 6 + i, device)
        for i, device in enumerate([] if k in whole else corners[h]):
            column = left + i * QUARTER
            forward(lambda column=column: piece(j, c, corner, 16, column, QUARTER), ns, nr, k * 6 + 4 + i, device)
        if k < 2:
            forward(held, ys, yr, k + 4, (y_up, y_down)[k])
        forward(held, gs, gr, k * 4, sib)

    def rest_y(k):
        j, h = steps[k]

        def held():
            return piece(j, c, wide, 32, h * HALF) if k in whole else piece(j, c, rest, 16, h * HALF)

        arrived(held(), ys.at[k + 6], yr.at[k + 6])
        if k < 2:
            forward(held, ys, yr, k + 10, (y_up, y_down)[k])
        forward(held, gs, gr, k * 4 + 3, sib)

    def from_around(k):
        j, h = steps[k]
        left = h * HALF
        for i in range(4):
            first = other_x if i < 2 else other_z
            n = k * 6 + i
            arrived(piece(j, c, first, 32, left + (i % 2) * QUARTER, QUARTER), ns.at[n], nr.at[n])
        forward(lambda: piece(j, c, other, 64, left), gs, gr, k * 4 + 1, sib)
        if k in whole:
            return
        for i in range(2):
            n = k * 6 + 4 + i
            arrived(piece(j, c, missing, 16, left + i * QUARTER, QUARTER), ns.at[n], nr.at[n])
        forward(lambda: piece(j, c, missing, 16, left), gs, gr, k * 4 + 2, sib)

    def from_sib(k):
        j, h = steps[k]
        parts = [(0, lead, 32), (1, other, 64)]
        parts += [(3, wide, 32)] if k in whole else [(2, missing, 16), (3, rest, 16)]
        for i, first, size in parts:
            arrived(piece(j, 1 - c, first, size, h * HALF), gs.at[k * 4 + i], gr.at[k * 4 + i])

    for k, (h, device) in enumerate([(0, y_up), (1, y_down), (1, y_up), (0, y_down)]):
        start_y(k, h, lead, 32, device)
    for k, (h, device) in enumerate([(0, y_up), (1, y_down)]):
        start_y(6 + k, h, rest, 16, device)

    def finish(j, acc):
        first = pl.multiple_of(j * CHUNK, CHUNK)
        here = pl.ds(first, CHUNK)

        low = acc[VOCAB:ROWS, :].astype(BF16)
        xr[:, here] = low
        e_buf[:, here] = acc[0:VOCAB, :] + jnp.dot(bl[...], low, preferred_element_type=F32)
        t_buf[:, here] = jnp.dot(bt2[...], low, preferred_element_type=F32)
        blocks = [pl.ds(i, BLOCK) for i in range(0, VOCAB, BLOCK)]

        def fold(values, add):
            return add(values.reshape(BLOCK // 8, 8, CHUNK), axis=0)

        top = fold(e_buf[blocks[0], here], jnp.max)
        for at in blocks[1:]:
            top = jnp.maximum(top, fold(e_buf[at, here], jnp.max))
        top = jnp.max(top, axis=0, keepdims=True)
        total = jnp.zeros((8, CHUNK), F32)
        weighted = jnp.zeros((8, CHUNK), F32)
        for at in blocks:
            e = jnp.exp(e_buf[at, here] - top)
            e_buf[at, here] = e
            h2[at, :] = e.astype(BF16)
            total = total + fold(e, jnp.sum)
            weighted = weighted + fold(e * t_buf[at, here], jnp.sum)
        total = jnp.sum(total, axis=0, keepdims=True)
        mean = jnp.sum(weighted, axis=0, keepdims=True) / total
        for at in blocks:
            h1[at, :] = (e_buf[at, here] * (t_buf[at, here] - mean)).astype(BF16)
        side, there = j // 2, pl.ds(pl.multiple_of((j % 2) * CHUNK, CHUNK), CHUNK)
        p0[side, 0:RANK, there] = jnp.dot(bt_ref[...], h1[...], preferred_element_type=F32)
        p0[side, RANK : 2 * RANK, there] = jnp.dot(bt_ref[...], h2[...], preferred_element_type=F32)
        p0[side, 2 * RANK : 2 * RANK + 8, there] = stat_rows(top, total, mean)

    for load in loads:
        load.wait()
    bt = bt_ref[...].astype(F32)
    dbt = dbt_ref[...].astype(F32)
    bl[...] = jnp.concatenate([bt, jnp.zeros_like(bt)], axis=0).T.astype(BF16)
    bt2[...] = jnp.concatenate([dbt, bt], axis=0).T.astype(BF16)

    def any_of(i, *values):
        hit = i == values[0]
        for value in values[1:]:
            hit = hit | (i == value)
        return hit

    def work(i, carry):
        @pl.when(i == 1)
        def _():
            from_y(0)
            from_y(1)
            start_y(8, 1, wide, 32, y_up)
            start_y(9, 0, wide, 32, y_down)

        @pl.when(i == 2)
        def _():
            from_y(2)
            from_y(3)
            rest_y(0)
            rest_y(1)
            from_around(0)
            from_around(1)
            from_y(4)
            from_y(5)
            from_sib(0)

        @pl.when(i == 3)
        def _():
            from_sib(1)

        @pl.when(i == 4)
        def _():
            rest_y(2)
            rest_y(3)
            from_around(2)
            from_around(3)
            from_sib(2)

        @pl.when(i == 5)
        def _():
            from_sib(3)

        @pl.when(i == 6)
        def _():
            from_sib(4)

        @pl.when(i == 7)
        def _():
            from_sib(5)

        step = jnp.where(i < 2, 0, jnp.where(any_of(i, 2, 4), 3, jnp.where(i < 6, 1, 2)))
        j = (y + step) % NY
        h = jnp.where(any_of(i, 1, 3, 4, 7), 1, 0)
        total = acc.at[jnp.where(step == 1, 1, 0)]
        here = pl.ds(pl.multiple_of(j * CHUNK, CHUNK), CHUNK)
        at = pl.ds(pl.multiple_of(h * HALF, 128), HALF)
        part = lax.dot_general(wall[:, at], sg[here, at], (((1,), (1,)), ((), ())), preferred_element_type=F32)
        fresh = any_of(i, 0, 2, 3, 6)

        @pl.when(fresh)
        def _():
            total[...] = part

        @pl.when(jnp.logical_not(fresh))
        def _():
            total[...] += part

        @pl.when(i == 4)
        def _():
            rest_y(4)
            rest_y(5)
            from_around(4)

        @pl.when(i == 5)
        def _():
            from_around(5)

        @pl.when(any_of(i, 1, 4, 5, 7))
        def _():
            finish(j, total)

        return carry

    lax.fori_loop(0, 8, work, 0)

    send(lambda: remote(p0.at[1 - c], r1, ss1.at[0], sr1.at[0], sib))
    arrived(r1, ss1.at[0], sr1.at[0])
    for tx in range(NX):
        lanes = pl.ds(tx * 128, 128)

        def stats(ref, row):
            return ref[pl.ds(row, 1), lanes]

        ours, theirs = p0.at[c], r1
        for ty in range(NY):
            g1, g2 = pl.ds(ty * 16, 16), pl.ds(RANK + ty * 16, 16)
            out = merge(
                [
                    (stats(ref, 128), stats(ref, 129), stats(ref, 130), ref[g1, lanes], ref[g2, lanes])
                    for ref in (ours, theirs)
                ]
            )
            p1[tx * NY + ty] = pack(*out)

    me = x * NY + y
    early = list(sends)
    sends.clear()
    for k, (px, py) in enumerate(xy):
        send(
            lambda k=k, px=px, py=py: remote(
                p1.at[px * NY + py], r2.at[me], xs.at[k], xrv.at[k], place(px, py, z, c)
            )
        )
    for make in early:
        make().wait_send()
    r2[me] = p1[me]
    for k, (dx, dy) in enumerate(pairs):
        origin = ((x - dx + NX) % NX) * NY + (y - dy + NY) % NY
        arrived(r2.at[origin], xs.at[k], xrv.at[k])
    out = merge([unpack(r2, k) for k in range(NX * NY)])
    r3[z] = pack(*out)
    for d in range(1, NZ):
        forward(lambda: r3.at[z], zs, zr, d - 1, place(x, y, (z + d) % NZ, c))
    for d in range(1, NZ):
        arrived(r3.at[(z - d + NZ) % NZ], zs.at[d - 1], zr.at[d - 1])
    top, total, mean, moved, plain = merge([unpack(r3, k) for k in range(NZ)])

    slot = c * NX + x
    strip = cg.at[slot, pl.ds(pl.multiple_of(y * 16, 16), 16)]
    strip[...] = (moved / total).astype(BF16)
    stg[slot] = stat_rows(top, total, mean)
    early = list(sends)
    sends.clear()
    for d in range(1, NX):
        forward(lambda: stg.at[slot], ts, tr, d - 1, place((x + d) % NX, y, z, c))
    for k, (px, py) in enumerate(xy):
        forward(lambda: strip, cs, cr, k, place(px, py, z, c))
    for make in early:
        make().wait_send()
    for d in range(1, NX):
        arrived(stg.at[c * NX + (x - d + NX) % NX], ts.at[d - 1], tr.at[d - 1])
    forward(lambda: stg.at[pl.ds(c * NX, NX)], fs, fr, 0, sib)

    def curve(core, first):
        tiles = [(pl.ds(pl.multiple_of(core * 512 + t * 128, 128), 128), core * NX + t) for t in range(NX)]
        factors, means = [], []
        for t, (lanes, k) in enumerate(tiles):
            local_top = p0[core, 2 * RANK : 2 * RANK + 1, t * 128 : (t + 1) * 128]
            factors.append(jnp.exp(local_top - stg[k, 0:1]) / stg[k, 1:2])
            means.append(stg[k, 2:3])

        def hessian(i, carry):
            at = pl.ds(pl.multiple_of(i * BLOCK, BLOCK), BLOCK)
            for t, (lanes, k) in enumerate(tiles):
                probs = e_buf[at, lanes] * factors[t]
                hs[at, lanes] = (probs * (t_buf[at, lanes] - means[t])).astype(BF16)
            return carry

        lax.fori_loop(0, VOCAB // BLOCK, hessian, 0)
        at = pl.ds(pl.multiple_of(core * 512, 512), 512)
        part = lax.dot_general(xr[0:RANK, at], hs[:, at], (((1,), (1,)), ((), ())), preferred_element_type=F32)
        gb_ref[...] = part if first else gb_ref[...] + part

    curve(c, True)
    for k, (dx, dy) in enumerate(pairs):
        at_x, at_y = (x - dx + NX) % NX, (y - dy + NY) % NY
        arrived(cg.at[c * NX + at_x, pl.ds(pl.multiple_of(at_y * 16, 16), 16)], cs.at[k], cr.at[k])
    forward(lambda: cg.at[pl.ds(c * NX, NX)], fs, fr, 1, sib)
    arrived(stg.at[pl.ds((1 - c) * NX, NX)], fs.at[0], fr.at[0])
    curve(1 - c, False)

    def outer(core, first):
        rows = pl.ds(pl.multiple_of(core * (TOKENS // 2), TOKENS // 2), TOKENS // 2)
        lows = jnp.concatenate([cg[core * NX + t] for t in range(NX)], axis=1)

        def columns(n, carry):
            at = pl.ds(pl.multiple_of(n * COLS, 128), COLS)
            part = jnp.dot(lows, sg[rows, at], preferred_element_type=F32)
            ga_ref[:, at] = part if first else ga_ref[:, at] + part
            return carry

        lax.fori_loop(0, WIDTH // COLS, columns, 0)

    outer(c, True)
    arrived(cg.at[pl.ds((1 - c) * NX, NX)], fs.at[1], fr.at[1])
    outer(1 - c, False)
    drain()


def shards(states, weight, first, second, first_direction, second_direction):
    vmem = pl.BlockSpec(memory_space=pltpu.VMEM)
    hbm = pl.BlockSpec(memory_space=pl.ANY)
    dma = pltpu.SemaphoreType.DMA
    grad_a, grad_b = pl.pallas_call(
        kernel,
        out_shape=(pltpu.VMEM((RANK, WIDTH), F32), pltpu.VMEM((RANK, VOCAB), F32)),
        in_specs=[hbm] * 6,
        out_specs=(vmem, vmem),
        scratch_shapes=[
            pltpu.VMEM((RANK, VOCAB), BF16),
            pltpu.VMEM((RANK, VOCAB), BF16),
            pltpu.VMEM((ROWS, WIDTH), BF16),
            pltpu.VMEM((TOKENS, WIDTH), BF16),
            pltpu.VMEM((2, ROWS, CHUNK), F32),
            pltpu.VMEM((VOCAB, TOKENS), F32),
            pltpu.VMEM((VOCAB, TOKENS), F32),
            pltpu.VMEM((2 * RANK, TOKENS), BF16),
            pltpu.VMEM((VOCAB, 2 * RANK), BF16),
            pltpu.VMEM((VOCAB, 2 * RANK), BF16),
            pltpu.VMEM((VOCAB, CHUNK), BF16),
            pltpu.VMEM((VOCAB, CHUNK), BF16),
            pltpu.VMEM((VOCAB, TOKENS), BF16),
            pltpu.VMEM((2, 2 * RANK + 8, TOKENS // 2), F32),
            pltpu.VMEM((2 * RANK + 8, TOKENS // 2), F32),
            pltpu.VMEM((NX * NY, 48, 128), BF16),
            pltpu.VMEM((NX * NY, 48, 128), BF16),
            pltpu.VMEM((NZ, 48, 128), BF16),
            pltpu.VMEM((2 * NX, RANK, 128), BF16),
            pltpu.VMEM((2 * NX, 8, 128), F32),
            dma((6,)),
            dma((12,)), dma((12,)),
            dma((36,)), dma((36,)),
            dma((24,)), dma((24,)),
            dma((1,)), dma((1,)),
            dma((15,)), dma((15,)),
            dma((7,)), dma((7,)),
            dma((15,)), dma((15,)),
            dma((3,)), dma((3,)),
            dma((2,)), dma((2,)),
        ],
        compiler_params=pltpu.CompilerParams(
            collective_id=0, has_side_effects=True, vmem_limit_bytes=56 * 1024 * 1024
        ),
        cost_estimate=pl.CostEstimate(flops=10_000_000_000, bytes_accessed=20_000_000, transcendentals=800_000),
    )(states, weight, first, first_direction, second.T, second_direction.T)
    return grad_a, grad_b.T


def solution(mesh):
    in_specs = (
        P("dp", None),
        P(("dp", "vocab"), None),
        P(),
        P(("dp", "vocab"), None),
        P(),
        P(("dp", "vocab"), None),
    )
    out_specs = (P(), P(("dp", "vocab"), None))
    return jax.shard_map(shards, mesh=mesh, in_specs=in_specs, out_specs=out_specs, check_vma=False)
```

```python
import jax
import jax.numpy as jnp
from jax import lax
from jax.experimental import pallas as pl
from jax.experimental.pallas import tpu as pltpu
from jax.sharding import PartitionSpec as P

MESH = pl.DeviceIdType.MESH
F32 = jnp.float32
BF16 = jnp.bfloat16

WIDTH = 4608
RANK = 64
VOCAB = 768
TOKENS = 1024
CHUNK = 256
ROWS = VOCAB + 2 * RANK
NX, NY, NZ = 4, 4, 8
HALF = 2304
QUARTER = 1152
BLOCK = 64
COLS = 2304


def place(x, y, z, c):
    return (y, x * 16 + z * 2 + c)


def remote(src, dst, send_sem, recv_sem, device):
    return pltpu.make_async_remote_copy(
        src_ref=src,
        dst_ref=dst,
        send_sem=send_sem,
        recv_sem=recv_sem,
        device_id=device,
        device_id_type=MESH,
    )


def merge(parts):
    top = parts[0][0]
    for part in parts[1:]:
        top = jnp.maximum(top, part[0])
    scales = [jnp.exp(part[0] - top) for part in parts]
    total = scales[0] * parts[0][1]
    weighted = total * parts[0][2]
    for scale, part in zip(scales[1:], parts[1:]):
        share = scale * part[1]
        total = total + share
        weighted = weighted + share * part[2]
    mean = weighted / total
    moved = None
    plain = None
    for scale, part in zip(scales, parts):
        shift = scale * (part[2] - mean)
        one = scale * part[3] + shift * part[4]
        two = scale * part[4]
        moved = one if moved is None else moved + one
        plain = two if plain is None else plain + two
    return top, total, mean, moved, plain


def stat_rows(top, total, mean):
    return jnp.concatenate([top, total, mean, jnp.zeros((5, top.shape[1]), F32)], axis=0)


def pack(top, total, mean, moved, plain):
    stats = jnp.concatenate([top, total, mean], axis=0)
    high = stats.astype(BF16).astype(F32)
    middle = (stats - high).astype(BF16).astype(F32)
    low = stats - high - middle
    blank = jnp.zeros((7, top.shape[1]), F32)
    return jnp.concatenate([moved, plain, high, middle, low, blank], axis=0).astype(BF16)


def unpack(ref, k):
    block = ref[k].astype(F32)
    stats = block[32:35] + block[35:38] + block[38:41]
    return stats[0:1], stats[1:2], stats[2:3], block[0:16], block[16:32]


def store(a_ref, b_ref, a_out, b_out, sems):
    copies = [
        pltpu.make_async_copy(a_ref, a_out, sems.at[0]),
        pltpu.make_async_copy(b_ref, b_out, sems.at[1]),
    ]
    for copy in copies:
        copy.start()
    for copy in copies:
        copy.wait()


def kernel(
    s_ref, w_ref, a_ref, ad_ref, bt_hbm, dbt_hbm, ga_ref, gb_ref,
    bt_ref, dbt_ref,
    wall, sg, acc, e_buf, t_buf, xr, bl, bt2, h1, h2, hs,
    p0, r1, p1, r2, r3, cg, stg,
    load_sem, ys, yr, ns, nr, gs, gr, ss1, sr1, xs, xrv, zs, zr, cs, cr, ts, tr, fs, fr,
):
    y = lax.axis_index("dp")
    v = lax.axis_index("vocab")
    x, z, c = v // 16, (v // 2) % 8, v % 2
    sib = place(x, y, z, 1 - c)
    y_up, y_down = place(x, (y + 1) % NY, z, c), place(x, (y + 3) % NY, z, c)
    pairs = [(dx, dy) for dx in range(NX) for dy in range(NY) if (dx, dy) != (0, 0)]
    xy = [((x + dx) % NX, (y + dy) % NY) for dx, dy in pairs]

    barrier = pltpu.get_barrier_semaphore()
    everyone = [y_up, y_down, sib]
    everyone += [place((x + dx) % NX, y, z, c) for dx in (1, 3)]
    everyone += [place(x, y, (z + d) % NZ, c) for d in range(1, NZ)]
    everyone += [place((x + dx) % NX, y, (z + dz) % NZ, c) for dx in (1, 3) for dz in (1, 7)]
    everyone += [place(px, py, z, c) for (dx, dy), (px, py) in zip(pairs, xy) if (dx, dy) not in ((0, 1), (0, 3), (1, 0), (3, 0))]
    for peer in everyone:
        pl.semaphore_signal(barrier, 1, device_id=peer, device_id_type=MESH)

    def rows_of(j, start, size):
        return sg.at[pl.ds(pl.multiple_of(j * CHUNK + start, 16), size)]

    loads = [
        pltpu.make_async_copy(s_ref, rows_of(y, 0, CHUNK), load_sem.at[0]),
        pltpu.make_async_copy(w_ref, wall.at[pl.ds(0, VOCAB)], load_sem.at[1]),
        pltpu.make_async_copy(a_ref, wall.at[pl.ds(VOCAB, RANK)], load_sem.at[2]),
        pltpu.make_async_copy(ad_ref, wall.at[pl.ds(VOCAB + RANK, RANK)], load_sem.at[3]),
        pltpu.make_async_copy(bt_hbm, bt_ref, load_sem.at[4]),
        pltpu.make_async_copy(dbt_hbm, dbt_ref, load_sem.at[5]),
    ]
    for load in loads:
        load.start()

    pl.semaphore_wait(barrier, len(everyone))

    odd = x % 2
    colour = (x + z) % 2
    lead, rest, wide = colour * 64 + odd * 32, colour * 64 + 32 - odd * 16, colour * 64 + 32 - odd * 32
    corner, missing = colour * 64 + odd * 48, colour * 64 + (1 - odd) * 48
    other = (1 - colour) * 64
    other_x, other_z = other + (1 - odd) * 32, other + odd * 32
    before, after, across = (y + 3) % NY, (y + 1) % NY, (y + 2) % NY
    whole = (2, 3)
    steps = [(before, 0), (after, 1), (before, 1), (after, 0), (across, 0), (across, 1)]
    around = [
        place((x + 1) % NX, y, z, c),
        place((x + 3) % NX, y, z, c),
        place(x, y, (z + 1) % NZ, c),
        place(x, y, (z + 7) % NZ, c),
    ]
    corners = [
        [place((x + 1) % NX, y, (z + 1) % NZ, c), place((x + 3) % NX, y, (z + 7) % NZ, c)],
        [place((x + 1) % NX, y, (z + 7) % NZ, c), place((x + 3) % NX, y, (z + 1) % NZ, c)],
    ]
    sends = []

    def send(make):
        make().start()
        sends.append(make)

    def drain():
        for make in sends:
            make().wait_send()
        sends.clear()

    def arrived(ref, send_sem, recv_sem):
        remote(ref, ref, send_sem, recv_sem, sib).wait_recv()

    def piece(j, core, first, size, column, width=HALF):
        row = pl.multiple_of(j * CHUNK + core * (CHUNK // 2) + first, 16)
        return sg.at[pl.ds(row, size), pl.ds(column, width)]

    def start_y(k, h, first, size, device):
        def make():
            row = pl.multiple_of(c * (CHUNK // 2) + first, 16)
            held = s_ref.at[pl.ds(row, size), pl.ds(h * HALF, HALF)]
            return remote(held, piece(y, c, first, size, h * HALF), ys.at[k], yr.at[k], device)

        send(make)

    def forward(pick, send_sems, recv_sems, n, device):
        send(lambda: remote(pick(), pick(), send_sems.at[n], recv_sems.at[n], device))

    def from_y(k):
        j, h = steps[k]
        left = h * HALF

        def held():
            return piece(j, c, lead, 32, left)

        arrived(held(), ys.at[k], yr.at[k])
        for i, device in enumerate(around):
            column = left + (i % 2) * QUARTER
            forward(lambda column=column: piece(j, c, lead, 32, column, QUARTER), ns, nr, k * 6 + i, device)
        for i, device in enumerate([] if k in whole else corners[h]):
            column = left + i * QUARTER
            forward(lambda column=column: piece(j, c, corner, 16, column, QUARTER), ns, nr, k * 6 + 4 + i, device)
        if k < 2:
            forward(held, ys, yr, k + 4, (y_up, y_down)[k])
        forward(held, gs, gr, k * 4, sib)

    def rest_y(k):
        j, h = steps[k]

        def held():
            return piece(j, c, wide, 32, h * HALF) if k in whole else piece(j, c, rest, 16, h * HALF)

        arrived(held(), ys.at[k + 6], yr.at[k + 6])
        if k < 2:
            forward(held, ys, yr, k + 10, (y_up, y_down)[k])
        forward(held, gs, gr, k * 4 + 3, sib)

    def from_around(k):
        j, h = steps[k]
        left = h * HALF
        for i in range(4):
            first = other_x if i < 2 else other_z
            n = k * 6 + i
            arrived(piece(j, c, first, 32, left + (i % 2) * QUARTER, QUARTER), ns.at[n], nr.at[n])
        forward(lambda: piece(j, c, other, 64, left), gs, gr, k * 4 + 1, sib)
        if k in whole:
            return
        for i in range(2):
            n = k * 6 + 4 + i
            arrived(piece(j, c, missing, 16, left + i * QUARTER, QUARTER), ns.at[n], nr.at[n])
        forward(lambda: piece(j, c, missing, 16, left), gs, gr, k * 4 + 2, sib)

    def from_sib(k):
        j, h = steps[k]
        parts = [(0, lead, 32), (1, other, 64)]
        parts += [(3, wide, 32)] if k in whole else [(2, missing, 16), (3, rest, 16)]
        for i, first, size in parts:
            arrived(piece(j, 1 - c, first, size, h * HALF), gs.at[k * 4 + i], gr.at[k * 4 + i])

    for k, (h, device) in enumerate([(0, y_up), (1, y_down), (1, y_up), (0, y_down)]):
        start_y(k, h, lead, 32, device)
    for k, (h, device) in enumerate([(0, y_up), (1, y_down)]):
        start_y(6 + k, h, rest, 16, device)

    def finish(j, acc):
        first = pl.multiple_of(j * CHUNK, CHUNK)
        here = pl.ds(first, CHUNK)

        low = acc[VOCAB:ROWS, :].astype(BF16)
        xr[:, here] = low
        e_buf[:, here] = acc[0:VOCAB, :] + jnp.dot(bl[...], low, preferred_element_type=F32)
        t_buf[:, here] = jnp.dot(bt2[...], low, preferred_element_type=F32)
        blocks = [pl.ds(i, BLOCK) for i in range(0, VOCAB, BLOCK)]

        def fold(values, add):
            return add(values.reshape(BLOCK // 8, 8, CHUNK), axis=0)

        top = fold(e_buf[blocks[0], here], jnp.max)
        for at in blocks[1:]:
            top = jnp.maximum(top, fold(e_buf[at, here], jnp.max))
        top = jnp.max(top, axis=0, keepdims=True)
        total = jnp.zeros((8, CHUNK), F32)
        weighted = jnp.zeros((8, CHUNK), F32)
        for at in blocks:
            e = jnp.exp(e_buf[at, here] - top)
            e_buf[at, here] = e
            h2[at, :] = e.astype(BF16)
            total = total + fold(e, jnp.sum)
            weighted = weighted + fold(e * t_buf[at, here], jnp.sum)
        total = jnp.sum(total, axis=0, keepdims=True)
        mean = jnp.sum(weighted, axis=0, keepdims=True) / total
        for at in blocks:
            h1[at, :] = (e_buf[at, here] * (t_buf[at, here] - mean)).astype(BF16)
        side, there = j // 2, pl.ds(pl.multiple_of((j % 2) * CHUNK, CHUNK), CHUNK)
        p0[side, 0:RANK, there] = jnp.dot(bt_ref[...], h1[...], preferred_element_type=F32)
        p0[side, RANK : 2 * RANK, there] = jnp.dot(bt_ref[...], h2[...], preferred_element_type=F32)
        p0[side, 2 * RANK : 2 * RANK + 8, there] = stat_rows(top, total, mean)

    for load in loads:
        load.wait()
    bt = bt_ref[...].astype(F32)
    dbt = dbt_ref[...].astype(F32)
    bl[...] = jnp.concatenate([bt, jnp.zeros_like(bt)], axis=0).T.astype(BF16)
    bt2[...] = jnp.concatenate([dbt, bt], axis=0).T.astype(BF16)

    def any_of(i, *values):
        hit = i == values[0]
        for value in values[1:]:
            hit = hit | (i == value)
        return hit

    def work(i, carry):
        @pl.when(i == 1)
        def _():
            from_y(0)
            from_y(1)
            start_y(8, 1, wide, 32, y_up)
            start_y(9, 0, wide, 32, y_down)

        @pl.when(i == 2)
        def _():
            from_y(2)
            from_y(3)
            rest_y(0)
            rest_y(1)
            from_around(0)
            from_around(1)
            from_y(4)
            from_y(5)
            from_sib(0)

        @pl.when(i == 3)
        def _():
            from_sib(1)

        @pl.when(i == 4)
        def _():
            rest_y(2)
            rest_y(3)
            from_around(2)
            from_around(3)
            from_sib(2)

        @pl.when(i == 5)
        def _():
            from_sib(3)

        @pl.when(i == 6)
        def _():
            from_sib(4)

        @pl.when(i == 7)
        def _():
            from_sib(5)

        step = jnp.where(i < 2, 0, jnp.where(any_of(i, 2, 4), 3, jnp.where(i < 6, 1, 2)))
        j = (y + step) % NY
        h = jnp.where(any_of(i, 1, 3, 4, 7), 1, 0)
        total = acc.at[jnp.where(step == 1, 1, 0)]
        here = pl.ds(pl.multiple_of(j * CHUNK, CHUNK), CHUNK)
        at = pl.ds(pl.multiple_of(h * HALF, 128), HALF)
        part = lax.dot_general(wall[:, at], sg[here, at], (((1,), (1,)), ((), ())), preferred_element_type=F32)
        fresh = any_of(i, 0, 2, 3, 6)

        @pl.when(fresh)
        def _():
            total[...] = part

        @pl.when(jnp.logical_not(fresh))
        def _():
            total[...] += part

        @pl.when(i == 4)
        def _():
            rest_y(4)
            rest_y(5)
            from_around(4)

        @pl.when(i == 5)
        def _():
            from_around(5)

        @pl.when(any_of(i, 1, 4, 5, 7))
        def _():
            finish(j, total)

        return carry

    lax.fori_loop(0, 8, work, 0)

    send(lambda: remote(p0.at[1 - c], r1, ss1.at[0], sr1.at[0], sib))
    arrived(r1, ss1.at[0], sr1.at[0])
    for tx in range(NX):
        lanes = pl.ds(tx * 128, 128)

        def stats(ref, row):
            return ref[pl.ds(row, 1), lanes]

        ours, theirs = p0.at[c], r1
        for ty in range(NY):
            g1, g2 = pl.ds(ty * 16, 16), pl.ds(RANK + ty * 16, 16)
            out = merge(
                [
                    (stats(ref, 128), stats(ref, 129), stats(ref, 130), ref[g1, lanes], ref[g2, lanes])
                    for ref in (ours, theirs)
                ]
            )
            p1[tx * NY + ty] = pack(*out)

    me = x * NY + y
    early = list(sends)
    sends.clear()
    for k, (px, py) in enumerate(xy):
        send(
            lambda k=k, px=px, py=py: remote(
                p1.at[px * NY + py], r2.at[me], xs.at[k], xrv.at[k], place(px, py, z, c)
            )
        )
    for make in early:
        make().wait_send()
    r2[me] = p1[me]
    for k, (dx, dy) in enumerate(pairs):
        origin = ((x - dx + NX) % NX) * NY + (y - dy + NY) % NY
        arrived(r2.at[origin], xs.at[k], xrv.at[k])
    out = merge([unpack(r2, k) for k in range(NX * NY)])
    r3[z] = pack(*out)
    for d in range(1, NZ):
        forward(lambda: r3.at[z], zs, zr, d - 1, place(x, y, (z + d) % NZ, c))
    for d in range(1, NZ):
        arrived(r3.at[(z - d + NZ) % NZ], zs.at[d - 1], zr.at[d - 1])
    top, total, mean, moved, plain = merge([unpack(r3, k) for k in range(NZ)])

    slot = c * NX + x
    strip = cg.at[slot, pl.ds(pl.multiple_of(y * 16, 16), 16)]
    strip[...] = (moved / total).astype(BF16)
    stg[slot] = stat_rows(top, total, mean)
    early = list(sends)
    sends.clear()
    for d in range(1, NX):
        forward(lambda: stg.at[slot], ts, tr, d - 1, place((x + d) % NX, y, z, c))
    for k, (px, py) in enumerate(xy):
        forward(lambda: strip, cs, cr, k, place(px, py, z, c))
    for make in early:
        make().wait_send()
    for d in range(1, NX):
        arrived(stg.at[c * NX + (x - d + NX) % NX], ts.at[d - 1], tr.at[d - 1])
    forward(lambda: stg.at[pl.ds(c * NX, NX)], fs, fr, 0, sib)

    def curve(core, first):
        tiles = [(pl.ds(pl.multiple_of(core * 512 + t * 128, 128), 128), core * NX + t) for t in range(NX)]
        factors, means = [], []
        for t, (lanes, k) in enumerate(tiles):
            local_top = p0[core, 2 * RANK : 2 * RANK + 1, t * 128 : (t + 1) * 128]
            factors.append(jnp.exp(local_top - stg[k, 0:1]) / stg[k, 1:2])
            means.append(stg[k, 2:3])

        def hessian(i, carry):
            at = pl.ds(pl.multiple_of(i * BLOCK, BLOCK), BLOCK)
            for t, (lanes, k) in enumerate(tiles):
                probs = e_buf[at, lanes] * factors[t]
                hs[at, lanes] = (probs * (t_buf[at, lanes] - means[t])).astype(BF16)
            return carry

        lax.fori_loop(0, VOCAB // BLOCK, hessian, 0)
        at = pl.ds(pl.multiple_of(core * 512, 512), 512)
        part = lax.dot_general(xr[0:RANK, at], hs[:, at], (((1,), (1,)), ((), ())), preferred_element_type=F32)
        gb_ref[...] = part if first else gb_ref[...] + part

    curve(c, True)
    for k, (dx, dy) in enumerate(pairs):
        at_x, at_y = (x - dx + NX) % NX, (y - dy + NY) % NY
        arrived(cg.at[c * NX + at_x, pl.ds(pl.multiple_of(at_y * 16, 16), 16)], cs.at[k], cr.at[k])
    forward(lambda: cg.at[pl.ds(c * NX, NX)], fs, fr, 1, sib)
    arrived(stg.at[pl.ds((1 - c) * NX, NX)], fs.at[0], fr.at[0])
    curve(1 - c, False)

    def outer(core, first):
        rows = pl.ds(pl.multiple_of(core * (TOKENS // 2), TOKENS // 2), TOKENS // 2)
        lows = jnp.concatenate([cg[core * NX + t] for t in range(NX)], axis=1)

        def columns(n, carry):
            at = pl.ds(pl.multiple_of(n * COLS, 128), COLS)
            part = jnp.dot(lows, sg[rows, at], preferred_element_type=F32)
            ga_ref[:, at] = part if first else ga_ref[:, at] + part
            return carry

        lax.fori_loop(0, WIDTH // COLS, columns, 0)

    outer(c, True)
    arrived(cg.at[pl.ds((1 - c) * NX, NX)], fs.at[1], fr.at[1])
    outer(1 - c, False)
    drain()


def shards(states, weight, first, second, first_direction, second_direction):
    vmem = pl.BlockSpec(memory_space=pltpu.VMEM)
    hbm = pl.BlockSpec(memory_space=pl.ANY)
    dma = pltpu.SemaphoreType.DMA
    grad_a, grad_b = pl.pallas_call(
        kernel,
        out_shape=(pltpu.VMEM((RANK, WIDTH), F32), pltpu.VMEM((RANK, VOCAB), F32)),
        in_specs=[hbm] * 6,
        out_specs=(vmem, vmem),
        scratch_shapes=[
            pltpu.VMEM((RANK, VOCAB), BF16),
            pltpu.VMEM((RANK, VOCAB), BF16),
            pltpu.VMEM((ROWS, WIDTH), BF16),
            pltpu.VMEM((TOKENS, WIDTH), BF16),
            pltpu.VMEM((2, ROWS, CHUNK), F32),
            pltpu.VMEM((VOCAB, TOKENS), F32),
            pltpu.VMEM((VOCAB, TOKENS), F32),
            pltpu.VMEM((2 * RANK, TOKENS), BF16),
            pltpu.VMEM((VOCAB, 2 * RANK), BF16),
            pltpu.VMEM((VOCAB, 2 * RANK), BF16),
            pltpu.VMEM((VOCAB, CHUNK), BF16),
            pltpu.VMEM((VOCAB, CHUNK), BF16),
            pltpu.VMEM((VOCAB, TOKENS), BF16),
            pltpu.VMEM((2, 2 * RANK + 8, TOKENS // 2), F32),
            pltpu.VMEM((2 * RANK + 8, TOKENS // 2), F32),
            pltpu.VMEM((NX * NY, 48, 128), BF16),
            pltpu.VMEM((NX * NY, 48, 128), BF16),
            pltpu.VMEM((NZ, 48, 128), BF16),
            pltpu.VMEM((2 * NX, RANK, 128), BF16),
            pltpu.VMEM((2 * NX, 8, 128), F32),
            dma((6,)),
            dma((12,)), dma((12,)),
            dma((36,)), dma((36,)),
            dma((24,)), dma((24,)),
            dma((1,)), dma((1,)),
            dma((15,)), dma((15,)),
            dma((7,)), dma((7,)),
            dma((15,)), dma((15,)),
            dma((3,)), dma((3,)),
            dma((2,)), dma((2,)),
        ],
        compiler_params=pltpu.CompilerParams(
            collective_id=0, has_side_effects=True, vmem_limit_bytes=56 * 1024 * 1024
        ),
        cost_estimate=pl.CostEstimate(flops=10_000_000_000, bytes_accessed=20_000_000, transcendentals=800_000),
    )(states, weight, first, first_direction, second.T, second_direction.T)
    return grad_a, grad_b.T


def solution(mesh):
    in_specs = (
        P("dp", None),
        P(("dp", "vocab"), None),
        P(),
        P(("dp", "vocab"), None),
        P(),
        P(("dp", "vocab"), None),
    )
    out_specs = (P(), P(("dp", "vocab"), None))
    return jax.shard_map(shards, mesh=mesh, in_specs=in_specs, out_specs=out_specs, check_vma=False)
```

```python
import jax
import jax.numpy as jnp
from jax import lax
from jax.experimental import pallas as pl
from jax.experimental.pallas import tpu as pltpu
from jax.sharding import PartitionSpec as P

MESH = pl.DeviceIdType.MESH
F32 = jnp.float32
BF16 = jnp.bfloat16

WIDTH = 4608
RANK = 64
VOCAB = 768
TOKENS = 1024
CHUNK = 256
ROWS = VOCAB + 2 * RANK
NX, NY, NZ = 4, 4, 8
HALF = 2304
QUARTER = 1152
BLOCK = 64
COLS = 2304


def place(x, y, z, c):
    return (y, x * 16 + z * 2 + c)


def remote(src, dst, send_sem, recv_sem, device):
    return pltpu.make_async_remote_copy(
        src_ref=src,
        dst_ref=dst,
        send_sem=send_sem,
        recv_sem=recv_sem,
        device_id=device,
        device_id_type=MESH,
    )


def merge(parts):
    top = parts[0][0]
    for part in parts[1:]:
        top = jnp.maximum(top, part[0])
    scales = [jnp.exp(part[0] - top) for part in parts]
    total = scales[0] * parts[0][1]
    weighted = total * parts[0][2]
    for scale, part in zip(scales[1:], parts[1:]):
        share = scale * part[1]
        total = total + share
        weighted = weighted + share * part[2]
    mean = weighted / total
    moved = None
    plain = None
    for scale, part in zip(scales, parts):
        shift = scale * (part[2] - mean)
        one = scale * part[3] + shift * part[4]
        two = scale * part[4]
        moved = one if moved is None else moved + one
        plain = two if plain is None else plain + two
    return top, total, mean, moved, plain


def stat_rows(top, total, mean):
    return jnp.concatenate([top, total, mean, jnp.zeros((5, top.shape[1]), F32)], axis=0)


def pack(top, total, mean, moved, plain):
    stats = jnp.concatenate([top, total, mean], axis=0)
    high = stats.astype(BF16).astype(F32)
    middle = (stats - high).astype(BF16).astype(F32)
    low = stats - high - middle
    blank = jnp.zeros((7, top.shape[1]), F32)
    return jnp.concatenate([moved, plain, high, middle, low, blank], axis=0).astype(BF16)


def unpack(ref, k):
    block = ref[k].astype(F32)
    stats = block[32:35] + block[35:38] + block[38:41]
    return stats[0:1], stats[1:2], stats[2:3], block[0:16], block[16:32]


def store(a_ref, b_ref, a_out, b_out, sems):
    copies = [
        pltpu.make_async_copy(a_ref, a_out, sems.at[0]),
        pltpu.make_async_copy(b_ref, b_out, sems.at[1]),
    ]
    for copy in copies:
        copy.start()
    for copy in copies:
        copy.wait()


def kernel(
    s_ref, w_ref, a_ref, ad_ref, bt_hbm, dbt_hbm, ga_ref, gb_ref,
    bt_ref, dbt_ref,
    wall, sg, acc, e_buf, t_buf, xr, bl, bt2, h1, h2, hs,
    p0, r1, p1, r2, r3, cg, stg,
    load_sem, ys, yr, ns, nr, gs, gr, ss1, sr1, xs, xrv, zs, zr, cs, cr, ts, tr, fs, fr,
):
    y = lax.axis_index("dp")
    v = lax.axis_index("vocab")
    x, z, c = v // 16, (v // 2) % 8, v % 2
    sib = place(x, y, z, 1 - c)
    y_up, y_down = place(x, (y + 1) % NY, z, c), place(x, (y + 3) % NY, z, c)
    pairs = [(dx, dy) for dx in range(NX) for dy in range(NY) if (dx, dy) != (0, 0)]
    pairs.sort(key=lambda pair: -min(pair[0], NX - pair[0]) - min(pair[1], NY - pair[1]))
    xy = [((x + dx) % NX, (y + dy) % NY) for dx, dy in pairs]

    barrier = pltpu.get_barrier_semaphore()
    everyone = [y_up, y_down, sib]
    everyone += [place((x + dx) % NX, y, z, c) for dx in (1, 3)]
    everyone += [place(x, y, (z + d) % NZ, c) for d in range(1, NZ)]
    everyone += [place((x + dx) % NX, y, (z + dz) % NZ, c) for dx in (1, 3) for dz in (1, 7)]
    everyone += [place(px, py, z, c) for (dx, dy), (px, py) in zip(pairs, xy) if (dx, dy) not in ((0, 1), (0, 3), (1, 0), (3, 0))]
    for peer in everyone:
        pl.semaphore_signal(barrier, 1, device_id=peer, device_id_type=MESH)

    def rows_of(j, start, size):
        return sg.at[pl.ds(pl.multiple_of(j * CHUNK + start, 16), size)]

    loads = [
        pltpu.make_async_copy(s_ref, rows_of(y, 0, CHUNK), load_sem.at[0]),
        pltpu.make_async_copy(w_ref, wall.at[pl.ds(0, VOCAB)], load_sem.at[1]),
        pltpu.make_async_copy(a_ref, wall.at[pl.ds(VOCAB, RANK)], load_sem.at[2]),
        pltpu.make_async_copy(ad_ref, wall.at[pl.ds(VOCAB + RANK, RANK)], load_sem.at[3]),
        pltpu.make_async_copy(bt_hbm, bt_ref, load_sem.at[4]),
        pltpu.make_async_copy(dbt_hbm, dbt_ref, load_sem.at[5]),
    ]
    for load in loads:
        load.start()

    pl.semaphore_wait(barrier, len(everyone))

    odd = x % 2
    colour = (x + z) % 2
    lead, rest, wide = colour * 64 + odd * 32, colour * 64 + 32 - odd * 16, colour * 64 + 32 - odd * 32
    corner, missing = colour * 64 + odd * 48, colour * 64 + (1 - odd) * 48
    other = (1 - colour) * 64
    other_x, other_z = other + (1 - odd) * 32, other + odd * 32
    before, after, across = (y + 3) % NY, (y + 1) % NY, (y + 2) % NY
    whole = (2, 3)
    steps = [(before, 0), (after, 1), (before, 1), (after, 0), (across, 0), (across, 1)]
    around = [
        place((x + 1) % NX, y, z, c),
        place((x + 3) % NX, y, z, c),
        place(x, y, (z + 1) % NZ, c),
        place(x, y, (z + 7) % NZ, c),
    ]
    corners = [
        [place((x + 1) % NX, y, (z + 1) % NZ, c), place((x + 3) % NX, y, (z + 7) % NZ, c)],
        [place((x + 1) % NX, y, (z + 7) % NZ, c), place((x + 3) % NX, y, (z + 1) % NZ, c)],
    ]
    sends = []

    def send(make):
        make().start()
        sends.append(make)

    def drain():
        for make in sends:
            make().wait_send()
        sends.clear()

    def arrived(ref, send_sem, recv_sem):
        remote(ref, ref, send_sem, recv_sem, sib).wait_recv()

    def piece(j, core, first, size, column, width=HALF):
        row = pl.multiple_of(j * CHUNK + core * (CHUNK // 2) + first, 16)
        return sg.at[pl.ds(row, size), pl.ds(column, width)]

    def start_y(k, h, first, size, device):
        def make():
            row = pl.multiple_of(c * (CHUNK // 2) + first, 16)
            held = s_ref.at[pl.ds(row, size), pl.ds(h * HALF, HALF)]
            return remote(held, piece(y, c, first, size, h * HALF), ys.at[k], yr.at[k], device)

        send(make)

    def forward(pick, send_sems, recv_sems, n, device):
        send(lambda: remote(pick(), pick(), send_sems.at[n], recv_sems.at[n], device))

    def from_y(k):
        j, h = steps[k]
        left = h * HALF

        def held():
            return piece(j, c, lead, 32, left)

        arrived(held(), ys.at[k], yr.at[k])
        for i, device in enumerate(around):
            column = left + (i % 2) * QUARTER
            forward(lambda column=column: piece(j, c, lead, 32, column, QUARTER), ns, nr, k * 6 + i, device)
        for i, device in enumerate([] if k in whole else corners[h]):
            column = left + i * QUARTER
            forward(lambda column=column: piece(j, c, corner, 16, column, QUARTER), ns, nr, k * 6 + 4 + i, device)
        if k < 2:
            forward(held, ys, yr, k + 4, (y_up, y_down)[k])
        forward(held, gs, gr, k * 4, sib)

    def rest_y(k):
        j, h = steps[k]

        def held():
            return piece(j, c, wide, 32, h * HALF) if k in whole else piece(j, c, rest, 16, h * HALF)

        arrived(held(), ys.at[k + 6], yr.at[k + 6])
        if k < 2:
            forward(held, ys, yr, k + 10, (y_up, y_down)[k])
        forward(held, gs, gr, k * 4 + 3, sib)

    def from_around(k):
        j, h = steps[k]
        left = h * HALF
        for i in range(4):
            first = other_x if i < 2 else other_z
            n = k * 6 + i
            arrived(piece(j, c, first, 32, left + (i % 2) * QUARTER, QUARTER), ns.at[n], nr.at[n])
        forward(lambda: piece(j, c, other, 64, left), gs, gr, k * 4 + 1, sib)
        if k in whole:
            return
        for i in range(2):
            n = k * 6 + 4 + i
            arrived(piece(j, c, missing, 16, left + i * QUARTER, QUARTER), ns.at[n], nr.at[n])
        forward(lambda: piece(j, c, missing, 16, left), gs, gr, k * 4 + 2, sib)

    def from_sib(k):
        j, h = steps[k]
        parts = [(0, lead, 32), (1, other, 64)]
        parts += [(3, wide, 32)] if k in whole else [(2, missing, 16), (3, rest, 16)]
        for i, first, size in parts:
            arrived(piece(j, 1 - c, first, size, h * HALF), gs.at[k * 4 + i], gr.at[k * 4 + i])

    for k, (h, device) in enumerate([(0, y_up), (1, y_down), (1, y_up), (0, y_down)]):
        start_y(k, h, lead, 32, device)
    for k, (h, device) in enumerate([(0, y_up), (1, y_down)]):
        start_y(6 + k, h, rest, 16, device)

    def finish(j, acc):
        first = pl.multiple_of(j * CHUNK, CHUNK)
        here = pl.ds(first, CHUNK)

        low = acc[VOCAB:ROWS, :].astype(BF16)
        xr[:, here] = low
        e_buf[:, here] = acc[0:VOCAB, :] + jnp.dot(bl[...], low, preferred_element_type=F32)
        t_buf[:, here] = jnp.dot(bt2[...], low, preferred_element_type=F32)
        blocks = [pl.ds(i, BLOCK) for i in range(0, VOCAB, BLOCK)]

        def fold(values, add):
            return add(values.reshape(BLOCK // 8, 8, CHUNK), axis=0)

        top = fold(e_buf[blocks[0], here], jnp.max)
        for at in blocks[1:]:
            top = jnp.maximum(top, fold(e_buf[at, here], jnp.max))
        top = jnp.max(top, axis=0, keepdims=True)
        total = jnp.zeros((8, CHUNK), F32)
        weighted = jnp.zeros((8, CHUNK), F32)
        for at in blocks:
            e = jnp.exp(e_buf[at, here] - top)
            e_buf[at, here] = e
            h2[at, :] = e.astype(BF16)
            total = total + fold(e, jnp.sum)
            weighted = weighted + fold(e * t_buf[at, here], jnp.sum)
        total = jnp.sum(total, axis=0, keepdims=True)
        mean = jnp.sum(weighted, axis=0, keepdims=True) / total
        for at in blocks:
            h1[at, :] = (e_buf[at, here] * (t_buf[at, here] - mean)).astype(BF16)
        side, there = j // 2, pl.ds(pl.multiple_of((j % 2) * CHUNK, CHUNK), CHUNK)
        p0[side, 0:RANK, there] = jnp.dot(bt_ref[...], h1[...], preferred_element_type=F32)
        p0[side, RANK : 2 * RANK, there] = jnp.dot(bt_ref[...], h2[...], preferred_element_type=F32)
        p0[side, 2 * RANK : 2 * RANK + 8, there] = stat_rows(top, total, mean)

    for load in loads:
        load.wait()
    bt = bt_ref[...].astype(F32)
    dbt = dbt_ref[...].astype(F32)
    bl[...] = jnp.concatenate([bt, jnp.zeros_like(bt)], axis=0).T.astype(BF16)
    bt2[...] = jnp.concatenate([dbt, bt], axis=0).T.astype(BF16)

    def any_of(i, *values):
        hit = i == values[0]
        for value in values[1:]:
            hit = hit | (i == value)
        return hit

    def work(i, carry):
        @pl.when(i == 1)
        def _():
            from_y(0)
            from_y(1)
            start_y(8, 1, wide, 32, y_up)
            start_y(9, 0, wide, 32, y_down)

        @pl.when(i == 2)
        def _():
            from_y(2)
            from_y(3)
            rest_y(0)
            rest_y(1)
            from_around(0)
            from_around(1)
            from_y(4)
            from_y(5)
            from_sib(0)

        @pl.when(i == 3)
        def _():
            from_sib(1)

        @pl.when(i == 4)
        def _():
            rest_y(2)
            rest_y(3)
            from_around(2)
            from_around(3)
            from_sib(2)

        @pl.when(i == 5)
        def _():
            from_sib(3)

        @pl.when(i == 6)
        def _():
            from_sib(4)

        @pl.when(i == 7)
        def _():
            from_sib(5)

        step = jnp.where(i < 2, 0, jnp.where(any_of(i, 2, 4), 3, jnp.where(i < 6, 1, 2)))
        j = (y + step) % NY
        h = jnp.where(any_of(i, 1, 3, 4, 7), 1, 0)
        total = acc.at[jnp.where(step == 1, 1, 0)]
        here = pl.ds(pl.multiple_of(j * CHUNK, CHUNK), CHUNK)
        at = pl.ds(pl.multiple_of(h * HALF, 128), HALF)
        part = lax.dot_general(wall[:, at], sg[here, at], (((1,), (1,)), ((), ())), preferred_element_type=F32)
        fresh = any_of(i, 0, 2, 3, 6)

        @pl.when(fresh)
        def _():
            total[...] = part

        @pl.when(jnp.logical_not(fresh))
        def _():
            total[...] += part

        @pl.when(i == 4)
        def _():
            rest_y(4)
            rest_y(5)
            from_around(4)

        @pl.when(i == 5)
        def _():
            from_around(5)

        @pl.when(any_of(i, 1, 4, 5, 7))
        def _():
            finish(j, total)

        return carry

    lax.fori_loop(0, 8, work, 0)

    send(lambda: remote(p0.at[1 - c], r1, ss1.at[0], sr1.at[0], sib))
    arrived(r1, ss1.at[0], sr1.at[0])
    for tx in range(NX):
        lanes = pl.ds(tx * 128, 128)

        def stats(ref, row):
            return ref[pl.ds(row, 1), lanes]

        ours, theirs = p0.at[c], r1
        for ty in range(NY):
            g1, g2 = pl.ds(ty * 16, 16), pl.ds(RANK + ty * 16, 16)
            out = merge(
                [
                    (stats(ref, 128), stats(ref, 129), stats(ref, 130), ref[g1, lanes], ref[g2, lanes])
                    for ref in (ours, theirs)
                ]
            )
            p1[tx * NY + ty] = pack(*out)

    me = x * NY + y
    early = list(sends)
    sends.clear()
    for k, (px, py) in enumerate(xy):
        send(
            lambda k=k, px=px, py=py: remote(
                p1.at[px * NY + py], r2.at[me], xs.at[k], xrv.at[k], place(px, py, z, c)
            )
        )
    for make in early:
        make().wait_send()
    r2[me] = p1[me]
    for k, (dx, dy) in enumerate(pairs):
        origin = ((x - dx + NX) % NX) * NY + (y - dy + NY) % NY
        arrived(r2.at[origin], xs.at[k], xrv.at[k])
    out = merge([unpack(r2, k) for k in range(NX * NY)])
    r3[z] = pack(*out)
    for d in (4, 3, 5, 2, 6, 1, 7):
        forward(lambda: r3.at[z], zs, zr, d - 1, place(x, y, (z + d) % NZ, c))
    for d in range(1, NZ):
        arrived(r3.at[(z - d + NZ) % NZ], zs.at[d - 1], zr.at[d - 1])
    top, total, mean, moved, plain = merge([unpack(r3, k) for k in range(NZ)])

    slot = c * NX + x
    strip = cg.at[slot, pl.ds(pl.multiple_of(y * 16, 16), 16)]
    strip[...] = (moved / total).astype(BF16)
    stg[slot] = stat_rows(top, total, mean)
    early = list(sends)
    sends.clear()
    for d in range(1, NX):
        forward(lambda: stg.at[slot], ts, tr, d - 1, place((x + d) % NX, y, z, c))
    for k, (px, py) in enumerate(xy):
        forward(lambda: strip, cs, cr, k, place(px, py, z, c))
    for make in early:
        make().wait_send()
    for d in range(1, NX):
        arrived(stg.at[c * NX + (x - d + NX) % NX], ts.at[d - 1], tr.at[d - 1])
    forward(lambda: stg.at[pl.ds(c * NX, NX)], fs, fr, 0, sib)

    def curve(core, first):
        tiles = [(pl.ds(pl.multiple_of(core * 512 + t * 128, 128), 128), core * NX + t) for t in range(NX)]
        factors, means = [], []
        for t, (lanes, k) in enumerate(tiles):
            local_top = p0[core, 2 * RANK : 2 * RANK + 1, t * 128 : (t + 1) * 128]
            factors.append(jnp.exp(local_top - stg[k, 0:1]) / stg[k, 1:2])
            means.append(stg[k, 2:3])

        def hessian(i, carry):
            at = pl.ds(pl.multiple_of(i * BLOCK, BLOCK), BLOCK)
            for t, (lanes, k) in enumerate(tiles):
                probs = e_buf[at, lanes] * factors[t]
                hs[at, lanes] = (probs * (t_buf[at, lanes] - means[t])).astype(BF16)
            return carry

        lax.fori_loop(0, VOCAB // BLOCK, hessian, 0)
        at = pl.ds(pl.multiple_of(core * 512, 512), 512)
        part = lax.dot_general(xr[0:RANK, at], hs[:, at], (((1,), (1,)), ((), ())), preferred_element_type=F32)
        gb_ref[...] = part if first else gb_ref[...] + part

    curve(c, True)
    for k, (dx, dy) in enumerate(pairs):
        at_x, at_y = (x - dx + NX) % NX, (y - dy + NY) % NY
        arrived(cg.at[c * NX + at_x, pl.ds(pl.multiple_of(at_y * 16, 16), 16)], cs.at[k], cr.at[k])
    forward(lambda: cg.at[pl.ds(c * NX, NX)], fs, fr, 1, sib)
    arrived(stg.at[pl.ds((1 - c) * NX, NX)], fs.at[0], fr.at[0])
    curve(1 - c, False)

    def outer(core, first):
        rows = pl.ds(pl.multiple_of(core * (TOKENS // 2), TOKENS // 2), TOKENS // 2)
        lows = jnp.concatenate([cg[core * NX + t] for t in range(NX)], axis=1)

        def columns(n, carry):
            at = pl.ds(pl.multiple_of(n * COLS, 128), COLS)
            part = jnp.dot(lows, sg[rows, at], preferred_element_type=F32)
            ga_ref[:, at] = part if first else ga_ref[:, at] + part
            return carry

        lax.fori_loop(0, WIDTH // COLS, columns, 0)

    outer(c, True)
    arrived(cg.at[pl.ds((1 - c) * NX, NX)], fs.at[1], fr.at[1])
    outer(1 - c, False)
    drain()


def shards(states, weight, first, second, first_direction, second_direction):
    vmem = pl.BlockSpec(memory_space=pltpu.VMEM)
    hbm = pl.BlockSpec(memory_space=pl.ANY)
    dma = pltpu.SemaphoreType.DMA
    grad_a, grad_b = pl.pallas_call(
        kernel,
        out_shape=(pltpu.VMEM((RANK, WIDTH), F32), pltpu.VMEM((RANK, VOCAB), F32)),
        in_specs=[hbm] * 6,
        out_specs=(vmem, vmem),
        scratch_shapes=[
            pltpu.VMEM((RANK, VOCAB), BF16),
            pltpu.VMEM((RANK, VOCAB), BF16),
            pltpu.VMEM((ROWS, WIDTH), BF16),
            pltpu.VMEM((TOKENS, WIDTH), BF16),
            pltpu.VMEM((2, ROWS, CHUNK), F32),
            pltpu.VMEM((VOCAB, TOKENS), F32),
            pltpu.VMEM((VOCAB, TOKENS), F32),
            pltpu.VMEM((2 * RANK, TOKENS), BF16),
            pltpu.VMEM((VOCAB, 2 * RANK), BF16),
            pltpu.VMEM((VOCAB, 2 * RANK), BF16),
            pltpu.VMEM((VOCAB, CHUNK), BF16),
            pltpu.VMEM((VOCAB, CHUNK), BF16),
            pltpu.VMEM((VOCAB, TOKENS), BF16),
            pltpu.VMEM((2, 2 * RANK + 8, TOKENS // 2), F32),
            pltpu.VMEM((2 * RANK + 8, TOKENS // 2), F32),
            pltpu.VMEM((NX * NY, 48, 128), BF16),
            pltpu.VMEM((NX * NY, 48, 128), BF16),
            pltpu.VMEM((NZ, 48, 128), BF16),
            pltpu.VMEM((2 * NX, RANK, 128), BF16),
            pltpu.VMEM((2 * NX, 8, 128), F32),
            dma((6,)),
            dma((12,)), dma((12,)),
            dma((36,)), dma((36,)),
            dma((24,)), dma((24,)),
            dma((1,)), dma((1,)),
            dma((15,)), dma((15,)),
            dma((7,)), dma((7,)),
            dma((15,)), dma((15,)),
            dma((3,)), dma((3,)),
            dma((2,)), dma((2,)),
        ],
        compiler_params=pltpu.CompilerParams(
            collective_id=0, has_side_effects=True, vmem_limit_bytes=56 * 1024 * 1024
        ),
        cost_estimate=pl.CostEstimate(flops=10_000_000_000, bytes_accessed=20_000_000, transcendentals=800_000),
    )(states, weight, first, first_direction, second.T, second_direction.T)
    return grad_a, grad_b.T


def solution(mesh):
    in_specs = (
        P("dp", None),
        P(("dp", "vocab"), None),
        P(),
        P(("dp", "vocab"), None),
        P(),
        P(("dp", "vocab"), None),
    )
    out_specs = (P(), P(("dp", "vocab"), None))
    return jax.shard_map(shards, mesh=mesh, in_specs=in_specs, out_specs=out_specs, check_vma=False)
```
